512 devices in a mesh: cache: 32 (over z, core), head: 16 (over x, y).
Axes of the slice: x: 4, y: 4, z: 16, core: 2. Of those that a mesh axis runs over, the one named last changes fastest.
Arguments:
- hidden: bfloat16 [16384, 8192], P('cache', 'head'), may hold values from -6 to 6
- slot_owner: int32 [64], P('cache'), may hold values from 0 to 31, as said below
- slot_rows: int32 [64], P('cache'), may hold values from 1 to 256
- new_hidden: bfloat16 [2, 32, 8192], P(None, None, 'cache'), may hold values from -9 to 9
- w_query: bfloat16 [8192, 4096], P('cache', 'head'), may hold values from -2 to 2
- w_key: bfloat16 [8192, 4096], P('cache', 'head'), may hold values from -1 to 1
- w_value: bfloat16 [8192, 4096], P('cache', 'head'), may hold values from -0.0625 to 0.0625
- w_out: bfloat16 [4096, 8192], P('head', 'cache'), may hold values from -0.1875 to 0.1875
Outputs:
- key_cache: bfloat16 [16384, 4096], P('cache', 'head')
- value_cache: bfloat16 [16384, 4096], P('cache', 'head')
- step_out: bfloat16 [2, 32, 8192], P(None, None, ('cache', 'head'))
The draws below stay inside these ranges and needn't reach their ends.
Inputs may be any that keep to these rules, and one draw needn't show every extreme that they name: `slot_owner`: every conversation owns at least one stored block.
All inputs are finite; a program needn't handle non-finite values.
Results may differ from the reference program's by a relative error of at most 0.035.
Values may be sent and summed in bfloat16 or wider, within the bound.
A program may use at most 64 MiB of HBM per device.

```python
import jax
import jax.numpy as jnp
from jax import lax

D = 8192
HD = 128
BLOCK = 256
STEPS = 2
HEADS = 32
KVW = 4096
CONV = 32
SLOTS_ALL = 64


def stored_rows(key):
    anchor = jax.random.fold_in(key, 101)

    def one_block(index):
        return jax.random.truncated_normal(jax.random.fold_in(anchor, index), -6.0, 6.0, (BLOCK, D), jnp.float32)
    blocks = jax.vmap(one_block)(jnp.arange(SLOTS_ALL))
    return blocks.reshape(SLOTS_ALL * BLOCK, D)


def owner_table(key):
    anchor = jax.random.fold_in(key, 202)
    first_pass = jax.random.permutation(jax.random.fold_in(anchor, 1), CONV)
    lower_pick = jax.random.randint(jax.random.fold_in(anchor, 2), (SLOTS_ALL - CONV,), 0, CONV)
    upper_pick = jax.random.randint(jax.random.fold_in(anchor, 3), (SLOTS_ALL - CONV,), 0, CONV)
    extra_owners = first_pass[jnp.minimum(lower_pick, upper_pick)]
    owners = jnp.concatenate([first_pass, extra_owners])
    shuffle = jax.random.permutation(jax.random.fold_in(anchor, 4), SLOTS_ALL)
    return owners[shuffle].astype(jnp.int32)


def key_base(key):
    return jax.random.truncated_normal(jax.random.fold_in(key, 505), -3.0, 3.0, (D, KVW), jnp.float32) * D ** (-0.5)


def draw_hidden(key, part):
    result = stored_rows(key)
    return result.astype(jnp.bfloat16)


def draw_slot_owner(key, part):
    return owner_table(key)


def draw_slot_rows(key, part):
    key = jax.random.fold_in(key, 303)
    partial_rows = jax.random.randint(jax.random.fold_in(key, 1), (SLOTS_ALL,), 1, BLOCK + 1)
    chooser = jax.random.randint(jax.random.fold_in(key, 2), (SLOTS_ALL,), 0, 4)
    counts = jnp.where(chooser == 0, partial_rows, BLOCK)
    counts = counts.at[0].set(BLOCK).at[1].set(1)
    return counts.astype(jnp.int32)


def draw_new_hidden(key, part):
    key = jax.random.fold_in(key, 404)
    result = jax.random.truncated_normal(key, -6.0, 6.0, (STEPS, CONV, D), jnp.float32)
    return result.astype(jnp.bfloat16)


def draw_w_key(key, part):
    result = key_base(key)
    return result.astype(jnp.bfloat16)


def draw_w_query(key, part):
    key = jax.random.fold_in(key, 606)
    own_part = jax.random.truncated_normal(key, -3.0, 3.0, (D, KVW), jnp.float32) * D ** (-0.5)
    result = own_part
    return result.astype(jnp.bfloat16)


def with_spikes(drawn, stream_key, source, target, parts, factor):
    def block_of(dim):
        return (jnp.arange(drawn.shape[dim]) // (drawn.shape[dim] // parts)).reshape((-1,) + (1,) * (drawn.ndim - 1 - dim))

    one_side = jax.random.permutation(stream_key, parts)[block_of(target)]
    other_side = (block_of(target) + parts // 2) % parts
    return jnp.where((block_of(source) == one_side) | (block_of(source) == other_side), factor * drawn, drawn)


def block_scale(stream_key, dims, cuts, low, high):
    loudness = 1.0
    for position, blocks in cuts:
        draws = jax.random.uniform(jax.random.fold_in(jax.random.fold_in(stream_key, 6), position), (blocks,), jnp.float32, low / len(cuts), high / len(cuts))
        loudness = loudness * jnp.repeat(jnp.exp(draws), dims[position] // blocks).reshape((-1,) + (1,) * (len(dims) - 1 - position))
    return loudness


def gaussian(own_key, extent, scale, limit, cuts=(), dtype=jnp.bfloat16):
    values = jax.random.normal(own_key, extent, jnp.float32) * scale
    if len(cuts) > 0:
        values = block_scale(own_key, extent, cuts, -0.22, 0.18) * values
    return jnp.clip(values, min=-limit, max=limit).astype(dtype)


def bell_draw_with(stream_key, dims, deviation, most, pieces, heavy, kind=jnp.bfloat16):
    drawn = deviation * jax.random.normal(stream_key, dims, jnp.float32)
    if pieces:
        drawn = drawn * block_scale(stream_key, dims, pieces, -0.22, 0.18)
    return jnp.clip(with_spikes(drawn, jax.random.fold_in(stream_key, 3), *heavy), -most, most).astype(kind)


def setup_inputs(seed: int = 0) -> dict:
    key_of = jax.random.split(jax.random.key(seed), 9)
    return {
        "hidden": draw_hidden(jax.random.fold_in(key_of[8], 71), 0),
        "slot_owner": draw_slot_owner(jax.random.fold_in(key_of[8], 71), 0),
        "slot_rows": draw_slot_rows(jax.random.fold_in(key_of[8], 71), 0),
        "new_hidden": draw_new_hidden(jax.random.fold_in(key_of[8], 71), 0),
        "w_query": draw_w_query(jax.random.fold_in(key_of[8], 71), 0),
        "w_key": draw_w_key(jax.random.fold_in(key_of[8], 71), 0),
        "w_value": gaussian(key_of[6], (D, KVW), D ** -0.5, 0.0625, ((0, 32), (1, 16))),
        "w_out": bell_draw_with(key_of[7], (KVW, D), KVW ** -0.5, 0.1875, ((0, 16), (1, 32)), (0, 1, 32, 2.75)),
    }


def reference(hidden, slot_owner, slot_rows, new_hidden, w_query, w_key, w_value, w_out):
    scale = HD ** -0.5
    within = jnp.arange(BLOCK)[None, :] < slot_rows[:, None]
    live_rows = within.reshape(SLOTS_ALL * BLOCK)
    live = live_rows.astype(jnp.float32)[:, None]
    key_cache = (jnp.dot(hidden, w_key, preferred_element_type=jnp.float32) * live).astype(jnp.bfloat16)
    value_cache = (jnp.dot(hidden, w_value, preferred_element_type=jnp.float32) * live).astype(jnp.bfloat16)
    row_owner = jnp.repeat(slot_owner, BLOCK)
    allowed = (row_owner[None, :] == jnp.arange(CONV)[:, None]) & live_rows[None, :]
    cache_keys = key_cache.astype(jnp.float32).reshape(SLOTS_ALL * BLOCK, HEADS, HD)
    cache_values = value_cache.astype(jnp.float32).reshape(SLOTS_ALL * BLOCK, HEADS, HD)
    tokens = new_hidden[0]
    fresh_keys = []
    fresh_values = []
    outputs = []
    for step_index in range(STEPS):
        query = jnp.dot(tokens, w_query, preferred_element_type=jnp.float32).astype(jnp.bfloat16)
        fresh_keys.append(jnp.dot(tokens, w_key, preferred_element_type=jnp.float32).astype(jnp.bfloat16))
        fresh_values.append(jnp.dot(tokens, w_value, preferred_element_type=jnp.float32).astype(jnp.bfloat16))
        query_wide = query.astype(jnp.float32).reshape(CONV, HEADS, HD)
        scores = jnp.einsum("chd,rhd->crh", query_wide, cache_keys) * scale
        scores = jnp.where(allowed[:, :, None], scores, -jnp.inf)
        new_keys = jnp.stack(fresh_keys).astype(jnp.float32).reshape(step_index + 1, CONV, HEADS, HD)
        new_values = jnp.stack(fresh_values).astype(jnp.float32).reshape(step_index + 1, CONV, HEADS, HD)
        new_scores = jnp.einsum("chd,tchd->cth", query_wide, new_keys) * scale
        peak = jnp.maximum(jnp.max(scores, axis=1), jnp.max(new_scores, axis=1))
        weights = jnp.exp(scores - peak[:, None, :])
        new_weights = jnp.exp(new_scores - peak[:, None, :])
        masses = jnp.sum(weights, axis=1) + jnp.sum(new_weights, axis=1)
        mixed = jnp.einsum("crh,rhd->chd", weights, cache_values, precision=lax.Precision.HIGHEST)
        mixed = mixed + jnp.einsum("cth,tchd->chd", new_weights, new_values, precision=lax.Precision.HIGHEST)
        attention = (mixed / masses[..., None]).reshape(CONV, KVW).astype(jnp.bfloat16)
        output = jnp.dot(attention, w_out, preferred_element_type=jnp.float32).astype(jnp.bfloat16)
        outputs.append(output)
        if step_index + 1 < STEPS:
            tokens = (new_hidden[step_index + 1].astype(jnp.float32) + output.astype(jnp.float32)).astype(jnp.bfloat16)
    return key_cache, value_cache, jnp.stack(outputs)
```

```python
import jax
import jax.numpy as jnp
from jax import lax
from jax.experimental import pallas as pl
from jax.experimental.pallas import tpu as pltpu
from jax.sharding import PartitionSpec as P

HD = 128
STEPS = 2
MESH = pl.DeviceIdType.MESH
NX, NY, NZ = 4, 4, 16
BLOCK = 256
QUARTER = 128


def place():
    c = lax.axis_index("cache")
    h = lax.axis_index("head")
    return c // 2, lax.rem(c, 2), h // NY, lax.rem(h, NY)


def at(z, k, x, y):
    return {"cache": z * 2 + k, "head": x * NY + y}


def hop(value, by, size):
    return lax.rem(value + (by + size), size)
Z_FAR_FIRST = (8, 7, -7, 6, -6, 5, -5, 4, -4, 3, -3, 2, -2, 1, -1)
PLANE_FAR_FIRST = tuple(
    sorted(
        ((dx, dy) for dx in (2, 1, -1, 0) for dy in (2, 1, -1, 0) if dx or dy),
        key=lambda d: -abs(d[0]) - abs(d[1]),
    )
)
K_NEW, K_WQ, K_WO, K_TAG_PAIR, K_TAG, K_OPAIR, K_OUT, K_LAST = range(8)
K_Q, K_KV, K_QPAIR, K_STATE, K_STATEPAIR = 8, 10, 12, 14, 16
KINDS = 18


def layer_kernel(
    owner_ref, rows_ref, hidden_ref, new_ref, wq_ref, wk_ref, wv_ref, wo_ref,
    key_ref, value_ref, out_ref,
    hbuf, wbuf, acc, kout, vout, fresh_in, wq2, wo2,
    qsend, qrecv, qpair, qall, kvsend, kvrecv, kvown, states, osend, orecv, opair, fsend, frecv,
    tags,
    hsend, hsem, wsend, wsem, sibsend, lsem, osem, msem, mrecv,
):
    z, k, x, y = place()
    me = x * NY + y
    mine = z * 2 + k
    xn = {s: at(z, k, hop(x, s, NX), y) for s in (1, -1)}
    yn = {s: at(z, k, x, hop(y, s, NY)) for s in (1, -1)}
    zn = {s: at(hop(z, s, NZ), k, x, y) for s in (1, -1)}
    sib = at(z, 1 - k, x, y)
    barrier = pltpu.get_barrier_semaphore()
    partners = [at(z, 1 - k, x, y)]
    partners += [at(hop(z, dz, NZ), k, x, y) for dz in Z_FAR_FIRST]
    partners += [at(z, k, hop(x, dx, NX), hop(y, dy, NY)) for dx, dy in PLANE_FAR_FIRST]
    for other in partners:
        pl.semaphore_signal(barrier, inc=1, device_id=other, device_id_type=MESH)
    local = [
        pltpu.make_async_copy(hidden_ref, hbuf.at[me], lsem.at[0]),
        pltpu.make_async_copy(wk_ref, wbuf.at[mine, 0], lsem.at[1]),
        pltpu.make_async_copy(wv_ref, wbuf.at[mine, 1], lsem.at[2]),
        pltpu.make_async_copy(new_ref, fresh_in.at[k], lsem.at[3]),
        pltpu.make_async_copy(wq_ref, wq2.at[k], lsem.at[4]),
        pltpu.make_async_copy(wo_ref, wo2.at[k], lsem.at[5]),
    ]
    for copy in local:
        copy.start()
    pl.semaphore_wait(barrier, len(partners))

    def source(dx, dy):
        return hop(x, dx, NX) * NY + hop(y, dy, NY)

    def push(dx, dy, piece, to, own=False):
        index = source(dx, dy)
        rows = pl.ds(piece * QUARTER, QUARTER)
        src = hidden_ref.at[rows] if own else hbuf.at[index, rows]
        pltpu.make_async_remote_copy(
            src_ref=src, dst_ref=hbuf.at[index, rows],
            send_sem=hsend, recv_sem=hsem.at[index, piece],
            device_id=to, device_id_type=MESH,
        ).start()

    def landed(dx, dy, pieces):
        index = source(dx, dy)
        for piece in pieces:
            part = hbuf.at[index, pl.ds(piece * QUARTER, QUARTER)]
            pltpu.make_async_copy(part, part, hsem.at[index, piece]).wait()

    def spread(half, a, b, axis, own=False):
        dx, dy = (a, b) if half == 0 else (b, a)
        nb = xn if axis == half else yn
        for sign in (1, -1):
            for piece in (2 * half, 2 * half + 1):
                push(dx, dy, piece, nb[sign], own)

    def relay(half, axis, other):
        nb = xn if axis == half else yn
        for sign, piece in ((1, 2 * half), (-1, 2 * half + 1)):
            step = (-sign, other) if axis == 0 else (other, -sign)
            dx, dy = step if half == 0 else step[::-1]
            push(dx, dy, piece, nb[sign])

    def got(half, a, b):
        dx, dy = (a, b) if half == 0 else (b, a)
        landed(dx, dy, (2 * half, 2 * half + 1))

    def hidden_round(r):
        for half in (0, 1):
            if r == 0:
                spread(half, 0, 0, 0, own=True)
        for half in (0, 1):
            if r == 0:
                spread(half, 0, 0, 1, own=True)
            if r == 1:
                got(half, 1, 0)
                got(half, -1, 0)
                relay(half, 0, 0)
                spread(half, -1, 0, 1)
                spread(half, 1, 0, 1)
            if r == 2:
                got(half, 0, 1)
                got(half, 0, -1)
                relay(half, 1, 0)
            if r == 3:
                got(half, 2, 0)
                spread(half, 2, 0, 1)
                got(half, 0, 2)
            if r == 4:
                got(half, -1, 1)
                got(half, -1, -1)
                relay(half, 1, -1)
            if r == 5:
                got(half, 1, 1)
                got(half, 1, -1)
                relay(half, 1, 1)
            if r == 6:
                got(half, 2, 1)
                got(half, 2, -1)
                relay(half, 1, 2)
            if r == 7:
                got(half, -1, 2)
                got(half, 1, 2)
            if r == 8:
                got(half, 2, 2)

    def ready(dx, dy):
        ax, ay = jnp.minimum(dx, NX - dx), jnp.minimum(dy, NY - dy)
        near = ax + ay
        both = jnp.where((dx == 3) & (dy == 3), 4, 5)
        far = jnp.where((ax == 2) & (ay == 2), 8, 7)
        out = jnp.where(near == 1, 2, jnp.where((ax == 0) | (ay == 0), 3, jnp.where(near == 2, both, far)))
        return jnp.where(near == 0, 0, out)

    def block(dz, core):
        return hop(z, dz, NZ) * 2 + core

    def ring(dz, chunk, to):
        part = wbuf.at[block(dz, k), chunk]
        src = (wk_ref if chunk == 0 else wv_ref) if dz == 0 else part
        pltpu.make_async_remote_copy(
            src_ref=src, dst_ref=part, send_sem=wsend, recv_sem=wsem.at[block(dz, k), chunk],
            device_id=to, device_id_type=MESH,
        ).start()

    def share(dz, chunk):
        part = wbuf.at[block(dz, k), chunk]
        src = (wk_ref if chunk == 0 else wv_ref) if dz == 0 else part
        pltpu.make_async_remote_copy(
            src_ref=src, dst_ref=part, send_sem=sibsend, recv_sem=wsem.at[block(dz, k), chunk],
            device_id=sib, device_id_type=MESH,
        ).start()

    def have(dz, core, chunk):
        part = wbuf.at[block(dz, core), chunk]
        pltpu.make_async_copy(part, part, wsem.at[block(dz, core), chunk]).wait()

    def weight_round(r):
        if r == 0:
            for chunk in (0, 1):
                for sign in (1, -1):
                    ring(0, chunk, zn[sign])
            for chunk in (0, 1):
                share(0, chunk)
        elif r < NZ // 2:
            for chunk in (0, 1):
                for sign in (1, -1):
                    have(-sign * r, k, chunk)
                    if r < NZ // 2 - 1 or (sign == 1) == (chunk == 0):
                        ring(-sign * r, chunk, zn[sign])
                    share(-sign * r, chunk)
        else:
            for chunk in (0, 1):
                have(r, k, chunk)
                share(r, chunk)

    def weight_settle(r):
        for dz in ((r, -r) if 0 < r < NZ // 2 else (r,)):
            for chunk in (0, 1):
                have(dz, 1 - k, chunk)

    def products(r, first):
        def one(h, carry):
            due = ready(hop(h // NY, NX - x, NX), hop(lax.rem(h, NY), NY - y, NY))
            away = hop(h, NZ - z, NZ)
            due = jnp.maximum(due, jnp.minimum(away, NZ - away))
            now = (due <= r) if first else (due == r)

            @pl.when(now)
            def _():
                for chunk in (0, 1):
                    part = jnp.dot(
                        hbuf[h, :, :BLOCK], wbuf[2 * h, chunk], preferred_element_type=jnp.float32
                    ) + jnp.dot(
                        hbuf[h, :, BLOCK:], wbuf[2 * h + 1, chunk], preferred_element_type=jnp.float32
                    )
                    acc[chunk] += part

            return carry

        lax.fori_loop(0, NX * NY, one, 0)

    def remote(src, dst, kind, to):
        pltpu.make_async_remote_copy(
            src_ref=src, dst_ref=dst, send_sem=msem.at[kind], recv_sem=mrecv.at[kind],
            device_id=to, device_id_type=MESH,
        ).start()

    def arrived(part, kind):
        pltpu.make_async_copy(part, part, mrecv.at[kind]).wait()

    def departed(part, kind):
        pltpu.make_async_copy(part, part, msem.at[kind]).wait()

    def along_z(src, dst, kind):
        for dz in Z_FAR_FIRST:
            remote(src, dst, kind, at(hop(z, dz, NZ), k, x, y))

    lane = lax.broadcasted_iota(jnp.int32, (1, 128), 1)
    my_row = (lax.broadcasted_iota(jnp.int32, (2, 128), 0) == k).astype(jnp.float32)

    def tag_row(values):
        row = jnp.zeros((1, 128), jnp.float32)
        for r, value in enumerate(values):
            row = jnp.where(lane == z * 8 + r, value, row)
        return row * my_row

    def pair_start():
        remote(new_ref, fresh_in.at[k], K_NEW, sib)
        remote(wq_ref, wq2.at[k], K_WQ, sib)
        remote(wo_ref, wo2.at[k], K_WO, sib)
        owners = [owner_ref[0].astype(jnp.float32), owner_ref[1].astype(jnp.float32)]
        tags[0, 6:8, :] = tag_row([owners[0], owners[0], owners[1], owners[1]])
        tags[0, 0:6, :] = jnp.zeros((6, 128), jnp.float32)
        remote(tags.at[0], tags.at[1], K_TAG_PAIR, sib)

    def pair_finish():
        arrived(fresh_in.at[k], K_NEW)
        arrived(wq2.at[k], K_WQ)
        arrived(wo2.at[k], K_WO)

    def owners_start():
        arrived(tags.at[1], K_TAG_PAIR)
        both = tags[0] + tags[1]
        tags[2] = both
        tags[3 + z] = both
        along_z(tags.at[2], tags.at[3 + z], K_TAG)

    def owners():
        total = jnp.sum(tags[3:], axis=0)
        row = jnp.concatenate([total[6:7], total[7:8]], axis=1)
        spot = lax.broadcasted_iota(jnp.int32, (1, 256), 1)
        kind = lax.rem(spot, 8)
        own = (spot // 8).astype(jnp.float32)
        return jnp.where(kind < 4, row, jnp.where(kind < 6, own, -1.0))

    def project(t, tokens):
        q = jnp.zeros((16, 256), jnp.float32)
        kv = [jnp.zeros((16, 256), jnp.float32)] * 2
        for core in (0, 1):
            q += jnp.dot(tokens[core], wq2[core], preferred_element_type=jnp.float32)
        q16 = q.astype(jnp.bfloat16)
        qsend[t] = q16
        qrecv[t, z] = q16
        along_z(qsend.at[t], qrecv.at[t, z], K_Q + t)
        for chunk in (0, 1):
            for core in (0, 1):
                kv[chunk] += jnp.dot(
                    tokens[core], wbuf[2 * z + core, chunk], preferred_element_type=jnp.float32
                )
        for chunk in (0, 1):
            for j in (0, 1):
                kvsend[t, :, 2 * chunk + j, :] = kv[chunk][:, j * HD : (j + 1) * HD]
        kvrecv[t, z] = kvsend[t, z]
        for dz in Z_FAR_FIRST:
            to = hop(z, dz, NZ)
            remote(kvsend.at[t, to], kvrecv.at[t, z], K_KV + t, at(to, k, x, y))

    def query_half(t):
        arrived(qrecv.at[t, pl.ds(0, 15)], K_Q + t)
        half = jnp.sum(qrecv[t].astype(jnp.float32), axis=0).astype(jnp.bfloat16)
        qpair[t, k] = half
        remote(qpair.at[t, k], qpair.at[t, k], K_QPAIR + t, sib)
        return half.astype(jnp.float32)

    def query_rest(t):
        arrived(qpair.at[t, 1 - k], K_QPAIR + t)
        qall[0:16, :] = qpair[t, 0].astype(jnp.float32)
        qall[16:32, :] = qpair[t, 1].astype(jnp.float32)

    def new_pair(t):
        arrived(kvrecv.at[t, pl.ds(0, 15)], K_KV + t)
        total = jnp.sum(kvrecv[t], axis=0)
        kvown[t] = total.astype(jnp.bfloat16).astype(jnp.float32)

    scale = HD ** (-0.5)
    sub2 = lax.broadcasted_iota(jnp.int32, (2, 128), 0)

    def new_state(t):
        q = qall[pl.ds(k * 16 + z, 1), :]
        q2 = jnp.where(sub2 == 0, q[:, :HD], q[:, HD:])
        scores = [
            jnp.sum(q2 * kvown[s, 0:2, :], axis=1, keepdims=True) * scale for s in range(t + 1)
        ]
        peak = scores[0]
        for s in scores[1:]:
            peak = jnp.maximum(peak, s)
        mass = jnp.zeros((2, 1), jnp.float32)
        mixed = jnp.zeros((2, HD), jnp.float32)
        for s, score in enumerate(scores):
            w = jnp.exp(score - peak)
            mass += w
            mixed += w * kvown[s, 2:4, :]
        return mixed / mass, peak + jnp.log(mass)

    def slot_state(i):
        rows = pl.ds(i * BLOCK, BLOCK)
        q = qall[pl.ds(owner_ref[i], 1), :]
        spot = lax.broadcasted_iota(jnp.int32, (8, 256), 1)
        line = lax.broadcasted_iota(jnp.int32, (8, 256), 0)
        q2 = jnp.where(spot // HD == line, q, 0.0).astype(jnp.bfloat16)
        scores = lax.dot_general(
            q2, kout[rows, :], (((1,), (1,)), ((), ())), preferred_element_type=jnp.float32
        )
        scores = jnp.where(spot < rows_ref[i], scores * scale, -1e30)
        peak = jnp.max(scores, axis=1, keepdims=True)
        w = jnp.exp(scores - peak)
        mass = jnp.sum(w, axis=1, keepdims=True)
        mixed = jnp.dot(w.astype(jnp.bfloat16), vout[rows, :], preferred_element_type=jnp.float32)
        mixed = mixed / mass
        lse = peak + jnp.log(mass)
        return jnp.where(sub2 == 0, mixed[0:2, :HD], mixed[0:2, HD:]), lse[0:2]

    def exchange_states(t):
        tag = []
        for i in range(3):
            mixed, lse = slot_state(i) if i < 2 else new_state(t)
            states[t, k, z, 2 * i : 2 * i + 2, :] = mixed
            tag += [lse[0:1], lse[1:2]]
        states[t, k, z, 6:8, :] = tag_row(tag)
        along_z(states.at[t, k, z], states.at[t, k, z], K_STATE + t)
        arrived(states.at[t, k, pl.ds(0, 15)], K_STATE + t)
        remote(states.at[t, k], states.at[t, k], K_STATEPAIR + t, sib)
        arrived(states.at[t, 1 - k], K_STATEPAIR + t)

    def attention(t, owner, first, count):
        held = states[t].reshape(256, 128)
        total = jnp.sum(states[t].reshape(32, 8, 128), axis=0)
        lse = jnp.concatenate([total[6:7], total[7:8]], axis=1)
        spot = lax.broadcasted_iota(jnp.int32, (count, 256), 1)
        conv = (lax.broadcasted_iota(jnp.int32, (count, 256), 0) + first).astype(jnp.float32)
        mine_ = owner == conv
        held = held.astype(jnp.bfloat16)
        parts = []
        for j in (0, 1):
            valid = mine_ & (lax.rem(spot, 2) == j)
            kept = jnp.where(valid, lse, -1e30)
            peak = jnp.max(kept, axis=1, keepdims=True)
            w = jnp.where(valid, jnp.exp(kept - peak), 0.0)
            w = w / jnp.sum(w, axis=1, keepdims=True)
            parts.append(
                jnp.dot(w.astype(jnp.bfloat16), held, preferred_element_type=jnp.float32)
            )
        return jnp.concatenate(parts, axis=1).astype(jnp.bfloat16)

    def plane(pick, dst, kind):
        for dx, dy in PLANE_FAR_FIRST:
            to = source(dx, dy)
            remote(pick(to), dst, kind, at(z, k, hop(x, dx, NX), hop(y, dy, NY)))

    def next_tokens(owner):
        half = attention(0, owner, 16 * k, 16)
        for core in (0, 1):
            part = jnp.dot(half, wo2[core], preferred_element_type=jnp.float32).astype(jnp.bfloat16)
            osend[core] = part
            orecv[me, core] = part
        plane(lambda to: osend, orecv.at[me], K_OUT)
        arrived(orecv.at[pl.ds(0, 15)], K_OUT)
        tokens = []
        for core in (0, 1):
            out = jnp.sum(orecv[:, core].astype(jnp.float32), axis=0).astype(jnp.bfloat16)
            opair[k, core] = out
            tokens.append(
                (fresh_in[core, 1, k].astype(jnp.float32) + out.astype(jnp.float32)).astype(
                    jnp.bfloat16
                )
            )
        return tokens

    def own_columns(value, width, start):
        pick = lax.broadcasted_iota(jnp.int32, (width, 16), 0) == (
            lax.broadcasted_iota(jnp.int32, (width, 16), 1) + start
        )
        return jnp.dot(
            value, pick.astype(jnp.bfloat16), preferred_element_type=jnp.float32
        ).astype(jnp.bfloat16)

    def last_output(owner):
        both = attention(1, owner, 0, 32)
        part = jnp.dot(both, wo2[k], preferred_element_type=jnp.float32).astype(jnp.bfloat16)
        for side in (0, 1):
            fsend[side] = part[:, side * 128 : (side + 1) * 128]
        frecv[me] = fsend[me // 8]
        plane(lambda to: fsend.at[to // 8], frecv.at[me], K_LAST)
        for half in (0, 1):
            out_ref[0, 16 * half : 16 * half + 16, :] = own_columns(opair[half, k], 256, me * 16)
        arrived(frecv.at[pl.ds(0, 15)], K_LAST)
        out = jnp.sum(frecv[...].astype(jnp.float32), axis=0).astype(jnp.bfloat16)
        out_ref[1] = own_columns(out, 128, lax.rem(me, 8) * 16)

    for chunk in (0, 1):
        acc[chunk] = jnp.zeros(acc.shape[1:], jnp.float32)
    for r in range(9):
        weight_round(r)
        hidden_round(r)
        if r == 0:
            pair_start()
            for copy in local:
                copy.wait()
            pair_finish()
        weight_settle(r)
        if r == 0:
            project(0, [fresh_in[0, 0, k], fresh_in[1, 0, k]])
            owners_start()
        if r == 4:
            query_half(0)
        if r == 5:
            query_rest(0)
            new_pair(0)
        if r == 6:
            arrived(tags.at[pl.ds(3, 15)], K_TAG)
        if r >= 2:
            products(r, r == 2)
    for slot in (0, 1):
        rows = pl.ds(slot * BLOCK, BLOCK)
        keep = lax.broadcasted_iota(jnp.int32, (BLOCK, BLOCK), 0) < rows_ref[slot]
        for chunk, out in ((0, kout), (1, vout)):
            out[rows, :] = jnp.where(keep, acc[chunk, rows, :], 0.0).astype(jnp.bfloat16)
    outs = [
        pltpu.make_async_copy(kout, key_ref, osem.at[0]),
        pltpu.make_async_copy(vout, value_ref, osem.at[1]),
    ]
    for copy in outs:
        copy.start()
    owner = owners()
    exchange_states(0)
    tokens = next_tokens(owner)
    project(1, tokens)
    remote(opair.at[k, 1 - k], opair.at[k, 1 - k], K_OPAIR, sib)
    query_half(1)
    new_pair(1)
    query_rest(1)
    exchange_states(1)
    arrived(opair.at[1 - k, k], K_OPAIR)
    last_output(owner)

    pltpu.make_async_copy(hbuf.at[pl.ds(0, 15)], hbuf.at[pl.ds(0, 15)], hsend).wait()
    pltpu.make_async_copy(wbuf.at[pl.ds(0, 15)], wbuf.at[pl.ds(0, 15)], wsend).wait()
    pltpu.make_async_copy(wbuf.at[pl.ds(0, 16)], wbuf.at[pl.ds(0, 16)], sibsend).wait()
    departed(fresh_in.at[k], K_NEW)
    departed(wq2.at[k], K_WQ)
    departed(wo2.at[k], K_WO)
    departed(tags.at[1], K_TAG_PAIR)
    departed(tags.at[pl.ds(3, 15)], K_TAG)
    departed(opair.at[k, 1 - k], K_OPAIR)
    for t in (0, 1):
        departed(qrecv.at[t, pl.ds(0, 15)], K_Q + t)
        departed(kvrecv.at[t, pl.ds(0, 15)], K_KV + t)
        departed(qpair.at[t, k], K_QPAIR + t)
        departed(states.at[t, k, pl.ds(0, 15)], K_STATE + t)
        departed(states.at[t, k], K_STATEPAIR + t)
    departed(orecv.at[pl.ds(0, 15)], K_OUT)
    departed(frecv.at[pl.ds(0, 15)], K_LAST)
    for copy in outs:
        copy.wait()


def layer(hidden, slot_owner, slot_rows, new_hidden, w_query, w_key, w_value, w_out):
    rows, width = hidden.shape
    cols = w_key.shape[1]
    bf16, f32 = jnp.bfloat16, jnp.float32
    any_ = pl.BlockSpec(memory_space=pl.ANY)
    smem = pl.BlockSpec(memory_space=pltpu.SMEM)
    caches = [jax.ShapeDtypeStruct((rows, cols), bf16)] * 2
    dma = pltpu.SemaphoreType.DMA
    return pl.pallas_call(
        layer_kernel,
        out_shape=caches + [jax.ShapeDtypeStruct((STEPS, 32, 16), bf16)],
        in_specs=[smem, smem] + [any_] * 6,
        out_specs=[any_, any_, pl.BlockSpec(memory_space=pltpu.VMEM)],
        scratch_shapes=[
            pltpu.VMEM((NX * NY, rows, width), bf16),
            pltpu.VMEM((2 * NZ, 2, BLOCK, cols), bf16),
            pltpu.VMEM((2, rows, cols), f32),
            pltpu.VMEM((rows, cols), bf16),
            pltpu.VMEM((rows, cols), bf16),
            pltpu.VMEM((2, STEPS, 2, 16, 256), bf16),
            pltpu.VMEM((2, 256, 256), bf16),
            pltpu.VMEM((2, 256, 256), bf16),
            pltpu.VMEM((STEPS, 16, 256), bf16),
            pltpu.VMEM((STEPS, NZ, 16, 256), bf16),
            pltpu.VMEM((STEPS, 2, 16, 256), bf16),
            pltpu.VMEM((32, 256), f32),
            pltpu.VMEM((STEPS, NZ, 4, 128), f32),
            pltpu.VMEM((STEPS, NZ, 4, 128), f32),
            pltpu.VMEM((STEPS, 4, 128), f32),
            pltpu.VMEM((STEPS, 2, NZ, 8, 128), f32),
            pltpu.VMEM((2, 16, 256), bf16),
            pltpu.VMEM((16, 2, 16, 256), bf16),
            pltpu.VMEM((2, 2, 16, 256), bf16),
            pltpu.VMEM((2, 32, 128), bf16),
            pltpu.VMEM((16, 32, 128), bf16),
            pltpu.VMEM((3 + NZ, 8, 128), f32),
            dma, dma((NX * NY, 4)), dma, dma((2 * NZ, 2)), dma, dma((6,)), dma((2,)),
            dma((KINDS,)), dma((KINDS,)),
        ],
        compiler_params=pltpu.CompilerParams(
            collective_id=0, has_side_effects=True, vmem_limit_bytes=48 << 20
        ),
        name="layer",
    )(
        slot_owner, slot_rows, hidden, new_hidden.reshape(STEPS, 2, 16, 256),
        w_query, w_key, w_value, w_out,
    )


def solution(mesh):
    in_specs = (
        P("cache", "head"),
        P("cache"),
        P("cache"),
        P(None, None, "cache"),
        P("cache", "head"),
        P("cache", "head"),
        P("cache", "head"),
        P("head", "cache"),
    )
    out_specs = (P("cache", "head"), P("cache", "head"), P(None, None, ("cache", "head")))

    def on_device(*arrays):
        return tuple(layer(*arrays))

    return jax.shard_map(
        on_device, mesh=mesh, in_specs=in_specs, out_specs=out_specs, check_vma=False
    )
```

```python
import jax
import jax.numpy as jnp
from jax import lax
from jax.experimental import pallas as pl
from jax.experimental.pallas import tpu as pltpu
from jax.sharding import PartitionSpec as P

HD = 128
STEPS = 2
MESH = pl.DeviceIdType.MESH
NX, NY, NZ = 4, 4, 16
BLOCK = 256
QUARTER = 128


def place():
    c = lax.axis_index("cache")
    h = lax.axis_index("head")
    return c // 2, lax.rem(c, 2), h // NY, lax.rem(h, NY)


def at(z, k, x, y):
    return {"cache": z * 2 + k, "head": x * NY + y}


def hop(value, by, size):
    return lax.rem(value + (by + size), size)
Z_FAR_FIRST = (8, 7, -7, 6, -6, 5, -5, 4, -4, 3, -3, 2, -2, 1, -1)
PLANE_FAR_FIRST = tuple(
    sorted(
        ((dx, dy) for dx in (2, 1, -1, 0) for dy in (2, 1, -1, 0) if dx or dy),
        key=lambda d: -abs(d[0]) - abs(d[1]),
    )
)
K_NEW, K_WQ, K_WO, K_OPAIR, K_OUT, K_LAST = range(6)
K_Q, K_KV, K_QPAIR, K_STATE, K_STATEPAIR = 6, 8, 10, 12, 14
KINDS = 16
PRODUCT_TICKS = (5, 7, 9, 11, 12, 13, 14, 15)
AHEAD = 3


def layer_kernel(
    owner_ref, rows_ref, hidden_ref, new_ref, wq_ref, wk_ref, wv_ref, wo_ref,
    key_ref, value_ref, out_ref,
    hbuf, wbuf, acc, kout, vout, fresh_in, wq2, wo2,
    qsend, qrecv, qpair, qall, kvsend, kvrecv, kvown, states, osend, orecv, opair, fsend, frecv,
    hsend, hsem, wsend, wsem, sibsend, lsem, osem, msem, mrecv, hellos,
):
    z, k, x, y = place()
    me = x * NY + y
    mine = z * 2 + k
    xn = {s: at(z, k, hop(x, s, NX), y) for s in (1, -1)}
    yn = {s: at(z, k, x, hop(y, s, NY)) for s in (1, -1)}
    zn = {s: at(hop(z, s, NZ), k, x, y) for s in (1, -1)}
    sib = at(z, 1 - k, x, y)
    barrier = pltpu.get_barrier_semaphore()
    partners = [sib, xn[1], xn[-1], yn[1], yn[-1], zn[1], zn[-1]]
    for other in partners:
        pl.semaphore_signal(barrier, inc=1, device_id=other, device_id_type=MESH)
    local = [
        pltpu.make_async_copy(hidden_ref, hbuf.at[me], lsem.at[0]),
        pltpu.make_async_copy(wk_ref, wbuf.at[mine, 0], lsem.at[1]),
        pltpu.make_async_copy(wv_ref, wbuf.at[mine, 1], lsem.at[2]),
        pltpu.make_async_copy(new_ref, fresh_in.at[k], lsem.at[3]),
        pltpu.make_async_copy(wq_ref, wq2.at[k], lsem.at[4]),
        pltpu.make_async_copy(wo_ref, wo2.at[k], lsem.at[5]),
    ]
    for copy in local:
        copy.start()
    pl.semaphore_wait(barrier, len(partners))

    def source(dx, dy):
        return hop(x, dx, NX) * NY + hop(y, dy, NY)

    def push(dx, dy, piece, to, own=False):
        index = source(dx, dy)
        rows = pl.ds(piece * QUARTER, QUARTER)
        src = hidden_ref.at[rows] if own else hbuf.at[index, rows]
        pltpu.make_async_remote_copy(
            src_ref=src, dst_ref=hbuf.at[index, rows],
            send_sem=hsend, recv_sem=hsem.at[index, piece],
            device_id=to, device_id_type=MESH,
        ).start()

    def landed(dx, dy, pieces):
        index = source(dx, dy)
        for piece in pieces:
            part = hbuf.at[index, pl.ds(piece * QUARTER, QUARTER)]
            pltpu.make_async_copy(part, part, hsem.at[index, piece]).wait()

    def piece_of(half, sign, turn):
        return 2 * half + (turn if sign == 1 else 1 - turn)

    SLOTS = {
        1: ("own", 0, 0), 2: ("own", 0, 1), 3: ("own", 1, 0), 4: ("own", 1, 1), 5: ("pass", 0, 0),
        6: (-1, 1, 0), 7: (-1, 1, 1), 8: (1, 1, 0), 9: (1, 1, 1), 10: ("pass", 1, 0),
        11: (2, 1, 0), 12: (2, 1, 1), 13: ("pass", 1, -1), 14: ("pass", 1, 1), 15: ("pass", 1, 2),
    }

    def hidden_slot(slot, arriving):
        what, axis, turn = SLOTS[slot]
        for half in (0, 1):
            nb = xn if axis == half else yn
            for sign in (1, -1):
                if what == "pass":
                    a, b = (-sign, 0) if axis == 0 else (turn, -sign)
                    piece = piece_of(half, sign, 0)
                    if arriving:
                        a, b = (2, 0) if axis == 0 else (turn, 2)
                else:
                    a, b = (0, 0) if what == "own" else (what, 0)
                    piece = piece_of(half, sign, turn)
                    if arriving:
                        a, b = (-sign, b) if axis == 0 else (a, -sign)
                dx, dy = (a, b) if half == 0 else (b, a)
                if arriving:
                    landed(dx, dy, (piece,))
                else:
                    push(dx, dy, piece, nb[sign], own=what == "own")

    def ready(dx, dy):
        ax, ay = jnp.minimum(dx, NX - dx), jnp.minimum(dy, NY - dy)
        near = ax + ay
        side = jnp.where((dx == 3) | (dy == 3), 13, 14)
        both = jnp.where((dx == 3) & (dy == 3), 7, 9)
        straight = jnp.where(near == 1, 4, 10)
        far = jnp.where(near == 4, 15, side)
        out = jnp.where(near == 2, both, far)
        out = jnp.where((ax == 0) | (ay == 0), straight, out)
        return jnp.where(near == 0, 0, out)

    def block(dz, core):
        return hop(z, dz, NZ) * 2 + core

    def ring(dz, chunk, part, to):
        rows = pl.ds(part * QUARTER, QUARTER)
        held = wbuf.at[block(dz, k), chunk, rows]
        src = (wk_ref if chunk == 0 else wv_ref).at[rows] if dz == 0 else held
        pltpu.make_async_remote_copy(
            src_ref=src, dst_ref=held, send_sem=wsend,
            recv_sem=wsem.at[block(dz, k), chunk, part],
            device_id=to, device_id_type=MESH,
        ).start()

    def share(dz, chunk):
        part = wbuf.at[block(dz, k), chunk]
        src = (wk_ref if chunk == 0 else wv_ref) if dz == 0 else part
        pltpu.make_async_remote_copy(
            src_ref=src, dst_ref=part, send_sem=sibsend, recv_sem=wsem.at[block(dz, k), chunk, 0],
            device_id=sib, device_id_type=MESH,
        ).start()

    def have(dz, core, chunk):
        part = wbuf.at[block(dz, core), chunk]
        pltpu.make_async_copy(part, part, wsem.at[block(dz, core), chunk, 0]).wait()

    def have_part(dz, chunk, part):
        held = wbuf.at[block(dz, k), chunk, pl.ds(part * QUARTER, QUARTER)]
        pltpu.make_async_copy(held, held, wsem.at[block(dz, k), chunk, part]).wait()

    def weight_slot(slot):
        r, chunk, part = (slot + 3) // 4, (slot - 1) % 4 // 2, (slot - 1) % 2
        if r < NZ // 2:
            for sign in (1, -1):
                have_part(-sign * r, chunk, part)
                if r < NZ // 2 - 1 or (sign == 1) == (chunk == 0):
                    ring(-sign * r, chunk, part, zn[sign])
        else:
            for chunk in (0, 1):
                have_part(NZ // 2, chunk, part)

    def hello(step):
        for side, sign in ((0, 1), (1, -1)):
            pl.semaphore_signal(hellos.at[side], inc=1, device_id=zn[sign], device_id_type=MESH)
        for side in (0, 1):
            pl.semaphore_wait(hellos.at[side], 1)

    def share_tick(tick):
        if tick == 0:
            for chunk in (0, 1):
                share(0, chunk)
        elif tick < NZ - 1:
            for sign in (1, -1):
                share(-sign * ((tick + 1) // 2), (tick + 1) % 2)
        else:
            for chunk in (0, 1):
                share(NZ // 2, chunk)

    def weight_settle(r):
        for dz in ((r, -r) if 0 < r < NZ // 2 else (r,)):
            for chunk in (0, 1):
                have(dz, 1 - k, chunk)

    def products(after, upto):
        def one(h, carry):
            due = ready(hop(h // NY, NX - x, NX), hop(lax.rem(h, NY), NY - y, NY))
            away = hop(h, NZ - z, NZ)
            due = jnp.maximum(due, jnp.minimum(2 * jnp.minimum(away, NZ - away), NZ - 1))
            now = (due > after) & (due <= upto)

            @pl.when(now)
            def _():
                for chunk in (0, 1):
                    part = jnp.dot(
                        hbuf[h, :, :BLOCK], wbuf[2 * h, chunk], preferred_element_type=jnp.float32
                    ) + jnp.dot(
                        hbuf[h, :, BLOCK:], wbuf[2 * h + 1, chunk], preferred_element_type=jnp.float32
                    )
                    acc[chunk] += part

            return carry

        lax.fori_loop(0, NX * NY, one, 0)

    def remote(src, dst, kind, to):
        pltpu.make_async_remote_copy(
            src_ref=src, dst_ref=dst, send_sem=msem.at[kind], recv_sem=mrecv.at[kind],
            device_id=to, device_id_type=MESH,
        ).start()

    def arrived(part, kind):
        pltpu.make_async_copy(part, part, mrecv.at[kind]).wait()

    def departed(part, kind):
        pltpu.make_async_copy(part, part, msem.at[kind]).wait()

    def along_z(src, dst, kind, part=slice(None)):
        for dz in Z_FAR_FIRST[part]:
            remote(src, dst, kind, at(hop(z, dz, NZ), k, x, y))

    lane = lax.broadcasted_iota(jnp.int32, (1, 128), 1)

    def tag_row(values):
        row = jnp.zeros((1, 128), jnp.float32)
        for r, value in enumerate(values):
            row = jnp.where(lane == z * 8 + r, value, row)
        return row

    def pair_start():
        remote(new_ref, fresh_in.at[k], K_NEW, sib)
        remote(wq_ref, wq2.at[k], K_WQ, sib)
        remote(wo_ref, wo2.at[k], K_WO, sib)

    def pair_finish():
        arrived(fresh_in.at[k], K_NEW)
        arrived(wq2.at[k], K_WQ)
        arrived(wo2.at[k], K_WO)

    def project_query(t, tokens):
        q = jnp.zeros((16, 256), jnp.float32)
        for core in (0, 1):
            q += jnp.dot(tokens[core], wq2[core], preferred_element_type=jnp.float32)
        q16 = q.astype(jnp.bfloat16)
        qsend[t] = q16
        qrecv[t, z] = q16

    def send_query(t, part=slice(None)):
        along_z(qsend.at[t], qrecv.at[t, z], K_Q + t, part)

    def project_new(t, tokens):
        for chunk in (0, 1):
            kv = jnp.zeros((16, 256), jnp.float32)
            for core in (0, 1):
                kv += jnp.dot(
                    tokens[core], wbuf[2 * z + core, chunk], preferred_element_type=jnp.float32
                )
            for j in (0, 1):
                kvsend[t, :, 2 * chunk + j, :] = kv[:, j * HD : (j + 1) * HD]

    def send_new(t, part=slice(None)):
        rows = pl.ds(0, 6 if t == 0 else 4)
        for dz in Z_FAR_FIRST[part]:
            to = hop(z, dz, NZ)
            remote(kvsend.at[t, to, rows], kvrecv.at[t, z, rows], K_KV + t, at(to, k, x, y))

    def project_first():
        tokens = [fresh_in[0, 0, k], fresh_in[1, 0, k]]
        project_new(0, tokens)
        q = jnp.zeros((16, 256), jnp.float32)
        for core in (0, 1):
            q += jnp.dot(tokens[core], wq2[core], preferred_element_type=jnp.float32)
        for j in (0, 1):
            kvsend[0, :, 4 + j, :] = q[:, j * HD : (j + 1) * HD]

    def query_first():
        new_pair(0)
        along_z(qall.at[k * 16 + z], qall.at[k * 16 + z], K_Q)

    def query_first_half():
        arrived(qall.at[pl.ds(0, 15)], K_Q)
        half = qall.at[pl.ds(k * 16, 16)]
        remote(half, half, K_QPAIR, sib)

    def query_first_rest():
        arrived(qall.at[pl.ds(0, 16)], K_QPAIR)

    def query_half(t):
        arrived(qrecv.at[t, pl.ds(0, 15)], K_Q + t)
        half = jnp.sum(qrecv[t].astype(jnp.float32), axis=0).astype(jnp.bfloat16)
        qpair[t, k] = half
        remote(qpair.at[t, k], qpair.at[t, k], K_QPAIR + t, sib)
        return half.astype(jnp.float32)

    def query_rest(t):
        arrived(qpair.at[t, 1 - k], K_QPAIR + t)
        for half in (0, 1):
            q = qpair[t, half].astype(jnp.float32)
            for j in (0, 1):
                qall[16 * half : 16 * half + 16, j, :] = q[:, j * HD : (j + 1) * HD]

    def new_pair(t):
        rows = 6 if t == 0 else 4
        kvrecv[t, z] = kvsend[t, z]
        arrived(kvrecv.at[t, pl.ds(0, 15), pl.ds(0, rows)], K_KV + t)
        total = jnp.sum(kvrecv[t, :, 0:rows, :], axis=0).astype(jnp.bfloat16).astype(jnp.float32)
        kvown[t] = total[0:4]
        if t == 0:
            qall[k * 16 + z] = total[4:6]

    scale = HD ** (-0.5)
    sub2 = lax.broadcasted_iota(jnp.int32, (2, 128), 0)

    def new_state(t):
        q2 = qall[k * 16 + z]
        scores = [
            jnp.sum(q2 * kvown[s, 0:2, :], axis=1, keepdims=True) * scale for s in range(t + 1)
        ]
        peak = scores[0]
        for s in scores[1:]:
            peak = jnp.maximum(peak, s)
        mass = jnp.zeros((2, 1), jnp.float32)
        mixed = jnp.zeros((2, HD), jnp.float32)
        for s, score in enumerate(scores):
            w = jnp.exp(score - peak)
            mass += w
            mixed += w * kvown[s, 2:4, :]
        return mixed / mass, peak + jnp.log(mass)

    def slot_state(i):
        rows = pl.ds(i * BLOCK, BLOCK)
        q = qall[owner_ref[i]]
        spot = lax.broadcasted_iota(jnp.int32, (8, 256), 1)
        line = lax.broadcasted_iota(jnp.int32, (8, 128), 0)
        q2 = jnp.concatenate(
            [jnp.where(line == j, q[j : j + 1], 0.0).astype(jnp.bfloat16) for j in (0, 1)], axis=1
        )
        scores = lax.dot_general(
            q2, kout[rows, :], (((1,), (1,)), ((), ())), preferred_element_type=jnp.float32
        )
        scores = jnp.where(spot < rows_ref[i], scores * scale, -1e30)
        peak = jnp.max(scores, axis=1, keepdims=True)
        w = jnp.exp(scores - peak)
        mass = jnp.sum(w, axis=1, keepdims=True)
        mixed = jnp.dot(w.astype(jnp.bfloat16), vout[rows, :], preferred_element_type=jnp.float32)
        mixed = mixed / mass
        lse = peak + jnp.log(mass)
        return jnp.where(sub2 == 0, mixed[0:2, :HD], mixed[0:2, HD:]), lse[0:2]

    def exchange_states(t):
        tag = []
        for i in range(3):
            mixed, lse = slot_state(i) if i < 2 else new_state(t)
            states[t, k, z, 2 * i : 2 * i + 2, :] = mixed
            tag += [lse[0:1], lse[1:2]]
        states[t, k, z, 6:7, :] = tag_row(tag)
        first, second = owner_ref[0].astype(jnp.float32), owner_ref[1].astype(jnp.float32)
        own = (k * 16 + z).astype(jnp.float32)
        states[t, k, z, 7:8, :] = tag_row([first, first, second, second, own, own, -1.0, -1.0])
        along_z(states.at[t, k, z], states.at[t, k, z], K_STATE + t)
        arrived(states.at[t, k, pl.ds(0, 15)], K_STATE + t)
        remote(states.at[t, k], states.at[t, k], K_STATEPAIR + t, sib)
        arrived(states.at[t, 1 - k], K_STATEPAIR + t)

    def attention(t, first, count):
        held = states[t].reshape(256, 128)
        total = [jnp.sum(states[t, core], axis=0) for core in (0, 1)]
        lse = jnp.concatenate([total[0][6:7], total[1][6:7]], axis=1)
        owner = jnp.concatenate([total[0][7:8], total[1][7:8]], axis=1)
        spot = lax.broadcasted_iota(jnp.int32, (count, 256), 1)
        conv = (lax.broadcasted_iota(jnp.int32, (count, 256), 0) + first).astype(jnp.float32)
        mine_ = owner == conv
        held = held.astype(jnp.bfloat16)
        parts = []
        for j in (0, 1):
            valid = mine_ & (lax.rem(spot, 2) == j)
            kept = jnp.where(valid, lse, -1e30)
            peak = jnp.max(kept, axis=1, keepdims=True)
            w = jnp.where(valid, jnp.exp(kept - peak), 0.0)
            w = w / jnp.sum(w, axis=1, keepdims=True)
            parts.append(
                jnp.dot(w.astype(jnp.bfloat16), held, preferred_element_type=jnp.float32)
            )
        return jnp.concatenate(parts, axis=1).astype(jnp.bfloat16)

    def plane(pick, dst, kind):
        for dx, dy in PLANE_FAR_FIRST:
            to = source(dx, dy)
            remote(pick(to), dst, kind, at(z, k, hop(x, dx, NX), hop(y, dy, NY)))

    def next_tokens():
        half = attention(0, 16 * k, 16)
        for core in (0, 1):
            part = jnp.dot(half, wo2[core], preferred_element_type=jnp.float32).astype(jnp.bfloat16)
            osend[core] = part
            orecv[me, core] = part
        plane(lambda to: osend, orecv.at[me], K_OUT)
        arrived(orecv.at[pl.ds(0, 15)], K_OUT)
        tokens = []
        for core in (0, 1):
            out = jnp.sum(orecv[:, core].astype(jnp.float32), axis=0).astype(jnp.bfloat16)
            opair[k, core] = out
            tokens.append(
                (fresh_in[core, 1, k].astype(jnp.float32) + out.astype(jnp.float32)).astype(
                    jnp.bfloat16
                )
            )
        return tokens

    def own_columns(value, width, start):
        pick = lax.broadcasted_iota(jnp.int32, (width, 16), 0) == (
            lax.broadcasted_iota(jnp.int32, (width, 16), 1) + start
        )
        return jnp.dot(
            value, pick.astype(jnp.bfloat16), preferred_element_type=jnp.float32
        ).astype(jnp.bfloat16)

    def last_output():
        both = attention(1, 0, 32)
        part = jnp.dot(both, wo2[k], preferred_element_type=jnp.float32).astype(jnp.bfloat16)
        for side in (0, 1):
            fsend[side] = part[:, side * 128 : (side + 1) * 128]
        frecv[me] = fsend[me // 8]
        plane(lambda to: fsend.at[to // 8], frecv.at[me], K_LAST)
        for half in (0, 1):
            out_ref[0, 16 * half : 16 * half + 16, :] = own_columns(opair[half, k], 256, me * 16)
        arrived(frecv.at[pl.ds(0, 15)], K_LAST)
        out = jnp.sum(frecv[...].astype(jnp.float32), axis=0).astype(jnp.bfloat16)
        out_ref[1] = own_columns(out, 128, lax.rem(me, 8) * 16)

    for chunk in (0, 1):
        acc[chunk] = jnp.zeros(acc.shape[1:], jnp.float32)
    settled = -1
    done = -1
    near, rest = slice(0, 8), slice(8, None)
    for tick in range(NZ):
        if tick == 0:
            for chunk in (0, 1):
                for part in (0, 1):
                    for sign in (1, -1):
                        ring(0, chunk, part, zn[sign])
                hidden_slot(1 + chunk, False)
            hidden_slot(3, False)
            share_tick(0)
            pair_start()
        else:
            weight_slot(2 * tick - 1)
            if tick <= 4:
                hello(2 * tick - 1)
            hidden_slot(tick, True)
            if tick + AHEAD < NZ:
                hidden_slot(tick + AHEAD, False)
            weight_slot(2 * tick)
            if tick <= 4:
                hello(2 * tick)
            share_tick(tick)
        if tick == 2:
            for copy in local:
                copy.wait()
            pair_finish()
            weight_settle(0)
            settled = 0
            project_first()
        if tick == 4:
            send_new(0, near)
        if tick == 5:
            send_new(0, rest)
        if tick == 9:
            query_first()
        if tick == 12:
            query_first_half()
        if tick == 13:
            query_first_rest()
        if tick in PRODUCT_TICKS:
            upto = tick if tick == NZ - 1 else tick - 1
            while settled < NZ // 2 and min(2 * (settled + 1), NZ - 1) <= upto:
                settled += 1
                weight_settle(settled)
            products(done, upto)
            done = upto
    for slot in (0, 1):
        rows = pl.ds(slot * BLOCK, BLOCK)
        keep = lax.broadcasted_iota(jnp.int32, (BLOCK, BLOCK), 0) < rows_ref[slot]
        for chunk, out in ((0, kout), (1, vout)):
            out[rows, :] = jnp.where(keep, acc[chunk, rows, :], 0.0).astype(jnp.bfloat16)
    outs = [
        pltpu.make_async_copy(kout, key_ref, osem.at[0]),
        pltpu.make_async_copy(vout, value_ref, osem.at[1]),
    ]
    for copy in outs:
        copy.start()
    exchange_states(0)
    tokens = next_tokens()
    project_query(1, tokens)
    send_query(1)
    project_new(1, tokens)
    send_new(1)
    remote(opair.at[k, 1 - k], opair.at[k, 1 - k], K_OPAIR, sib)
    query_half(1)
    new_pair(1)
    departed(qall.at[pl.ds(0, 15)], K_Q)
    departed(qall.at[pl.ds(0, 16)], K_QPAIR)
    query_rest(1)
    exchange_states(1)
    arrived(opair.at[1 - k, k], K_OPAIR)
    last_output()

    pltpu.make_async_copy(hbuf.at[pl.ds(0, 15)], hbuf.at[pl.ds(0, 15)], hsend).wait()
    pltpu.make_async_copy(wbuf.at[pl.ds(0, 15)], wbuf.at[pl.ds(0, 15)], wsend).wait()
    pltpu.make_async_copy(wbuf.at[pl.ds(0, 16)], wbuf.at[pl.ds(0, 16)], sibsend).wait()
    departed(fresh_in.at[k], K_NEW)
    departed(wq2.at[k], K_WQ)
    departed(wo2.at[k], K_WO)
    departed(opair.at[k, 1 - k], K_OPAIR)
    departed(kvrecv.at[0, pl.ds(0, 15), pl.ds(0, 6)], K_KV)
    departed(qrecv.at[1, pl.ds(0, 15)], K_Q + 1)
    departed(kvrecv.at[1, pl.ds(0, 15), pl.ds(0, 4)], K_KV + 1)
    departed(qpair.at[1, k], K_QPAIR + 1)
    for t in (0, 1):
        departed(states.at[t, k, pl.ds(0, 15)], K_STATE + t)
        departed(states.at[t, k], K_STATEPAIR + t)
    departed(orecv.at[pl.ds(0, 15)], K_OUT)
    departed(frecv.at[pl.ds(0, 15)], K_LAST)
    for copy in outs:
        copy.wait()


def layer(hidden, slot_owner, slot_rows, new_hidden, w_query, w_key, w_value, w_out):
    rows, width = hidden.shape
    cols = w_key.shape[1]
    bf16, f32 = jnp.bfloat16, jnp.float32
    any_ = pl.BlockSpec(memory_space=pl.ANY)
    hbm = pl.BlockSpec(memory_space=pltpu.HBM)
    smem = pl.BlockSpec(memory_space=pltpu.SMEM)
    caches = [jax.ShapeDtypeStruct((rows, cols), bf16)] * 2
    dma = pltpu.SemaphoreType.DMA
    return pl.pallas_call(
        layer_kernel,
        out_shape=caches + [jax.ShapeDtypeStruct((STEPS, 32, 16), bf16)],
        in_specs=[smem, smem] + [hbm] * 6,
        out_specs=[any_, any_, pl.BlockSpec(memory_space=pltpu.VMEM)],
        scratch_shapes=[
            pltpu.VMEM((NX * NY, rows, width), bf16),
            pltpu.VMEM((2 * NZ, 2, BLOCK, cols), bf16),
            pltpu.VMEM((2, rows, cols), f32),
            pltpu.VMEM((rows, cols), bf16),
            pltpu.VMEM((rows, cols), bf16),
            pltpu.VMEM((2, STEPS, 2, 16, 256), bf16),
            pltpu.VMEM((2, 256, 256), bf16),
            pltpu.VMEM((2, 256, 256), bf16),
            pltpu.VMEM((STEPS, 16, 256), bf16),
            pltpu.VMEM((STEPS, NZ, 16, 256), bf16),
            pltpu.VMEM((STEPS, 2, 16, 256), bf16),
            pltpu.VMEM((32, 2, 128), f32),
            pltpu.VMEM((STEPS, NZ, 8, 128), f32),
            pltpu.VMEM((STEPS, NZ, 8, 128), f32),
            pltpu.VMEM((STEPS, 4, 128), f32),
            pltpu.VMEM((STEPS, 2, NZ, 8, 128), f32),
            pltpu.VMEM((2, 16, 256), bf16),
            pltpu.VMEM((16, 2, 16, 256), bf16),
            pltpu.VMEM((2, 2, 16, 256), bf16),
            pltpu.VMEM((2, 32, 128), bf16),
            pltpu.VMEM((16, 32, 128), bf16),
            dma, dma((NX * NY, 4)), dma, dma((2 * NZ, 2, 2)), dma, dma((6,)), dma((2,)),
            dma((KINDS,)), dma((KINDS,)), pltpu.SemaphoreType.REGULAR((2,)),
        ],
        compiler_params=pltpu.CompilerParams(
            collective_id=0, has_side_effects=True, vmem_limit_bytes=60 << 20
        ),
        name="layer",
    )(
        slot_owner, slot_rows, hidden, new_hidden.reshape(STEPS, 2, 16, 256),
        w_query, w_key, w_value, w_out,
    )


def solution(mesh):
    in_specs = (
        P("cache", "head"),
        P("cache"),
        P("cache"),
        P(None, None, "cache"),
        P("cache", "head"),
        P("cache", "head"),
        P("cache", "head"),
        P("head", "cache"),
    )
    out_specs = (P("cache", "head"), P("cache", "head"), P(None, None, ("cache", "head")))

    def on_device(*arrays):
        return tuple(layer(*arrays))

    return jax.shard_map(
        on_device, mesh=mesh, in_specs=in_specs, out_specs=out_specs, check_vma=False
    )
```

```python
import jax
import jax.numpy as jnp
from jax import lax
from jax.experimental import pallas as pl
from jax.experimental.pallas import tpu as pltpu
from jax.sharding import PartitionSpec as P

HD = 128
STEPS = 2
MESH = pl.DeviceIdType.MESH
NX, NY, NZ = 4, 4, 16
BLOCK = 256
QUARTER = 128


def place():
    c = lax.axis_index("cache")
    h = lax.axis_index("head")
    return c // 2, lax.rem(c, 2), h // NY, lax.rem(h, NY)


def at(z, k, x, y):
    return {"cache": z * 2 + k, "head": x * NY + y}


def hop(value, by, size):
    return lax.rem(value + (by + size), size)
Z_FAR_FIRST = (8, 7, -7, 6, -6, 5, -5, 4, -4, 3, -3, 2, -2, 1, -1)
PLANE_FAR_FIRST = tuple(
    sorted(
        ((dx, dy) for dx in (2, 1, -1, 0) for dy in (2, 1, -1, 0) if dx or dy),
        key=lambda d: -abs(d[0]) - abs(d[1]),
    )
)
K_NEW, K_WQ, K_WO, K_OPAIR, K_OUT, K_LAST = range(6)
K_Q, K_KV, K_QPAIR, K_STATE, K_STATEPAIR = 6, 8, 10, 12, 14
KINDS = 16
PRODUCT_TICKS = (5, 7, 9, 11, 12, 13, 14)
AHEAD = 3


def layer_kernel(
    owner_ref, rows_ref, hidden_ref, new_ref, wq_ref, wk_ref, wv_ref, wo_ref,
    key_ref, value_ref, out_ref,
    hbuf, wbuf, acc, kout, vout, fresh_in, wq2, wo2,
    qsend, qrecv, qpair, qall, kvsend, kvrecv, kvown, states, osend, orecv, opair, fsend, frecv,
    hsend, hsem, wsend, wsem, sibsend, lsem, osem, msem, mrecv, hellos,
):
    z, k, x, y = place()
    me = x * NY + y
    mine = z * 2 + k
    xn = {s: at(z, k, hop(x, s, NX), y) for s in (1, -1)}
    yn = {s: at(z, k, x, hop(y, s, NY)) for s in (1, -1)}
    zn = {s: at(hop(z, s, NZ), k, x, y) for s in (1, -1)}
    sib = at(z, 1 - k, x, y)
    barrier = pltpu.get_barrier_semaphore()
    partners = [sib, xn[1], xn[-1], yn[1], yn[-1], zn[1], zn[-1]]
    for other in partners:
        pl.semaphore_signal(barrier, inc=1, device_id=other, device_id_type=MESH)
    local = [
        pltpu.make_async_copy(hidden_ref, hbuf.at[me], lsem.at[0]),
        pltpu.make_async_copy(wk_ref, wbuf.at[mine, 0], lsem.at[1]),
        pltpu.make_async_copy(wv_ref, wbuf.at[mine, 1], lsem.at[2]),
        pltpu.make_async_copy(new_ref, fresh_in.at[k], lsem.at[3]),
        pltpu.make_async_copy(wq_ref, wq2.at[k], lsem.at[4]),
        pltpu.make_async_copy(wo_ref, wo2.at[k], lsem.at[5]),
    ]
    for copy in local:
        copy.start()
    pl.semaphore_wait(barrier, len(partners))

    def source(dx, dy):
        return hop(x, dx, NX) * NY + hop(y, dy, NY)

    def push(dx, dy, piece, to, own=False):
        index = source(dx, dy)
        rows = pl.ds(piece * QUARTER, QUARTER)
        src = hidden_ref.at[rows] if own else hbuf.at[index, rows]
        pltpu.make_async_remote_copy(
            src_ref=src, dst_ref=hbuf.at[index, rows],
            send_sem=hsend, recv_sem=hsem.at[index, piece],
            device_id=to, device_id_type=MESH,
        ).start()

    def landed(dx, dy, pieces):
        index = source(dx, dy)
        for piece in pieces:
            part = hbuf.at[index, pl.ds(piece * QUARTER, QUARTER)]
            pltpu.make_async_copy(part, part, hsem.at[index, piece]).wait()

    def piece_of(half, sign, turn):
        return 2 * half + (turn if sign == 1 else 1 - turn)

    SLOTS = {
        1: ("own", 0, 0), 2: ("own", 0, 1), 3: ("own", 1, 0), 4: ("own", 1, 1), 5: ("pass", 0, 0),
        6: (-1, 1, 0), 7: (-1, 1, 1), 8: (1, 1, 0), 9: (1, 1, 1), 10: ("pass", 1, 0),
        11: (2, 1, 0), 12: (2, 1, 1), 13: ("pass", 1, -1), 14: ("pass", 1, 1), 15: ("pass", 1, 2),
    }

    def hidden_slot(slot, arriving):
        what, axis, turn = SLOTS[slot]
        for half in (0, 1):
            nb = xn if axis == half else yn
            for sign in (1, -1):
                if what == "pass":
                    a, b = (-sign, 0) if axis == 0 else (turn, -sign)
                    piece = piece_of(half, sign, 0)
                    if arriving:
                        a, b = (2, 0) if axis == 0 else (turn, 2)
                else:
                    a, b = (0, 0) if what == "own" else (what, 0)
                    piece = piece_of(half, sign, turn)
                    if arriving:
                        a, b = (-sign, b) if axis == 0 else (a, -sign)
                dx, dy = (a, b) if half == 0 else (b, a)
                if arriving:
                    landed(dx, dy, (piece,))
                else:
                    push(dx, dy, piece, nb[sign], own=what == "own")

    def ready(dx, dy):
        ax, ay = jnp.minimum(dx, NX - dx), jnp.minimum(dy, NY - dy)
        near = ax + ay
        side = jnp.where((dx == 3) | (dy == 3), 13, 14)
        both = jnp.where((dx == 3) & (dy == 3), 7, 9)
        straight = jnp.where(near == 1, 4, 10)
        far = jnp.where(near == 4, 15, side)
        out = jnp.where(near == 2, both, far)
        out = jnp.where((ax == 0) | (ay == 0), straight, out)
        return jnp.where(near == 0, 0, out)

    def block(dz, core):
        return hop(z, dz, NZ) * 2 + core

    def ring(dz, chunk, part, to):
        rows = pl.ds(part * QUARTER, QUARTER)
        held = wbuf.at[block(dz, k), chunk, rows]
        src = (wk_ref if chunk == 0 else wv_ref).at[rows] if dz == 0 else held
        pltpu.make_async_remote_copy(
            src_ref=src, dst_ref=held, send_sem=wsend,
            recv_sem=wsem.at[block(dz, k), chunk, part],
            device_id=to, device_id_type=MESH,
        ).start()

    def share(dz, chunk, part=None):
        held, sem = wbuf.at[block(dz, k), chunk], wsem.at[block(dz, k), chunk, part or 0]
        src = (wk_ref if chunk == 0 else wv_ref) if dz == 0 else held
        if part is not None:
            held = held.at[pl.ds(part * QUARTER, QUARTER)]
            src = held
        pltpu.make_async_remote_copy(
            src_ref=src, dst_ref=held, send_sem=sibsend, recv_sem=sem,
            device_id=sib, device_id_type=MESH,
        ).start()

    def have(dz, core, chunk):
        part = wbuf.at[block(dz, core), chunk]
        pltpu.make_async_copy(part, part, wsem.at[block(dz, core), chunk, 0]).wait()

    def have_part(dz, chunk, part, core=k):
        held = wbuf.at[block(dz, core), chunk, pl.ds(part * QUARTER, QUARTER)]
        pltpu.make_async_copy(held, held, wsem.at[block(dz, core), chunk, part]).wait()

    def weight_slot(slot):
        r, chunk, part = (slot + 3) // 4, (slot - 1) % 4 // 2, (slot - 1) % 2
        if r < NZ // 2:
            for sign in (1, -1):
                have_part(-sign * r, chunk, part)
                if r < NZ // 2 - 1 or (sign == 1) == (chunk == 0):
                    ring(-sign * r, chunk, part, zn[sign])
        else:
            for chunk in (0, 1):
                have_part(NZ // 2, chunk, part)
                share(NZ // 2, chunk, part)

    def hello():
        for side, sign in ((0, 1), (1, -1)):
            pl.semaphore_signal(hellos.at[side], inc=1, device_id=zn[sign], device_id_type=MESH)

    def heard():
        for side in (0, 1):
            pl.semaphore_wait(hellos.at[side], 1)

    def share_tick(tick):
        if tick == 0:
            for chunk in (0, 1):
                share(0, chunk)
        elif tick < NZ - 1:
            for sign in (1, -1):
                share(-sign * ((tick + 1) // 2), (tick + 1) % 2)

    def weight_settle(r):
        for dz in ((r, -r) if 0 < r < NZ // 2 else (r,)):
            for chunk in (0, 1):
                have(dz, 1 - k, chunk)

    def add(h, cores):
        for chunk in (0, 1):
            part = None
            for core in cores:
                term = jnp.dot(
                    hbuf[h, :, pl.ds(core * BLOCK, BLOCK)], wbuf[2 * h + core, chunk],
                    preferred_element_type=jnp.float32,
                )
                part = term if part is None else part + term
            acc[chunk] += part

    def last_products():
        corner, across = source(2, 2), hop(z, NZ // 2, NZ)

        @pl.when(corner != across)
        def _():
            add(corner, (0, 1))

        for core in (0, 1):
            @pl.when(k == core)
            def _():
                add(across, (core,))

        for part in (0, 1):
            for chunk in (0, 1):
                have_part(NZ // 2, chunk, part, 1 - k)
        for core in (0, 1):
            @pl.when(k != core)
            def _():
                add(across, (core,))

    def products(after, upto):
        def one(h, carry):
            due = ready(hop(h // NY, NX - x, NX), hop(lax.rem(h, NY), NY - y, NY))
            away = hop(h, NZ - z, NZ)
            due = jnp.maximum(due, jnp.minimum(2 * jnp.minimum(away, NZ - away), NZ - 1))
            now = (due > after) & (due <= upto)

            @pl.when(now)
            def _():
                add(h, (0, 1))

            return carry

        lax.fori_loop(0, NX * NY, one, 0)

    def remote(src, dst, kind, to):
        pltpu.make_async_remote_copy(
            src_ref=src, dst_ref=dst, send_sem=msem.at[kind], recv_sem=mrecv.at[kind],
            device_id=to, device_id_type=MESH,
        ).start()

    def arrived(part, kind):
        pltpu.make_async_copy(part, part, mrecv.at[kind]).wait()

    def departed(part, kind):
        pltpu.make_async_copy(part, part, msem.at[kind]).wait()

    def each_z(send):
        def one(i, carry):
            d = NZ // 2 - (i + 1) // 2
            send(hop(z, jnp.where(lax.rem(i, 2) == 1, d, -d), NZ))
            return carry

        lax.fori_loop(0, NZ - 1, one, 0)

    def along_z(src, dst, kind):
        each_z(lambda to: remote(src, dst, kind, at(to, k, x, y)))

    lane = lax.broadcasted_iota(jnp.int32, (1, 128), 1)

    def tag_row(values):
        row = jnp.zeros((1, 128), jnp.float32)
        for r, value in enumerate(values):
            row = jnp.where(lane == z * 8 + r, value, row)
        return row

    def pair_start():
        remote(new_ref, fresh_in.at[k], K_NEW, sib)
        remote(wq_ref, wq2.at[k], K_WQ, sib)
        remote(wo_ref, wo2.at[k], K_WO, sib)

    def pair_finish():
        arrived(fresh_in.at[k], K_NEW)
        arrived(wq2.at[k], K_WQ)
        arrived(wo2.at[k], K_WO)

    def project_query(t, tokens):
        q = jnp.zeros((16, 256), jnp.float32)
        for core in (0, 1):
            q += jnp.dot(tokens[core], wq2[core], preferred_element_type=jnp.float32)
        q16 = q.astype(jnp.bfloat16)
        qsend[t] = q16
        qrecv[t, z] = q16

    def send_query(t):
        along_z(qsend.at[t], qrecv.at[t, z], K_Q + t)

    def project_new(t, tokens):
        for chunk in (0, 1):
            kv = jnp.zeros((16, 256), jnp.float32)
            for core in (0, 1):
                kv += jnp.dot(
                    tokens[core], wbuf[2 * z + core, chunk], preferred_element_type=jnp.float32
                )
            for j in (0, 1):
                kvsend[t, :, 2 * chunk + j, :] = kv[:, j * HD : (j + 1) * HD]

    def send_new(t, offsets=None):
        rows = pl.ds(0, 6 if t == 0 else 4)

        def send(to):
            remote(kvsend.at[t, to, rows], kvrecv.at[t, z, rows], K_KV + t, at(to, k, x, y))

        if offsets is None:
            each_z(send)
        else:
            for dz in offsets:
                send(hop(z, dz, NZ))

    def project_first():
        tokens = [fresh_in[0, 0, k], fresh_in[1, 0, k]]
        project_new(0, tokens)
        q = jnp.zeros((16, 256), jnp.float32)
        for core in (0, 1):
            q += jnp.dot(tokens[core], wq2[core], preferred_element_type=jnp.float32)
        for j in (0, 1):
            kvsend[0, :, 4 + j, :] = q[:, j * HD : (j + 1) * HD]

    def query_first():
        new_pair(0)
        along_z(qall.at[k * 16 + z], qall.at[k * 16 + z], K_Q)

    def query_first_half():
        arrived(qall.at[pl.ds(0, 15)], K_Q)
        half = qall.at[pl.ds(k * 16, 16)]
        remote(half, half, K_QPAIR, sib)

    def query_first_rest():
        arrived(qall.at[pl.ds(0, 16)], K_QPAIR)

    def query_half(t):
        arrived(qrecv.at[t, pl.ds(0, 15)], K_Q + t)
        half = jnp.sum(qrecv[t].astype(jnp.float32), axis=0).astype(jnp.bfloat16)
        qpair[t, k] = half
        remote(qpair.at[t, k], qpair.at[t, k], K_QPAIR + t, sib)
        return half.astype(jnp.float32)

    def query_rest(t):
        arrived(qpair.at[t, 1 - k], K_QPAIR + t)
        for half in (0, 1):
            q = qpair[t, half].astype(jnp.float32)
            for j in (0, 1):
                qall[16 * half : 16 * half + 16, j, :] = q[:, j * HD : (j + 1) * HD]

    def new_pair(t):
        rows = 6 if t == 0 else 4
        kvrecv[t, z] = kvsend[t, z]
        arrived(kvrecv.at[t, pl.ds(0, 15), pl.ds(0, rows)], K_KV + t)
        total = jnp.sum(kvrecv[t, :, 0:rows, :], axis=0).astype(jnp.bfloat16).astype(jnp.float32)
        kvown[t] = total[0:4]
        if t == 0:
            qall[k * 16 + z] = total[4:6]

    scale = HD ** (-0.5)
    sub2 = lax.broadcasted_iota(jnp.int32, (2, 128), 0)

    def new_state(t):
        q2 = qall[k * 16 + z]
        scores = [
            jnp.sum(q2 * kvown[s, 0:2, :], axis=1, keepdims=True) * scale for s in range(t + 1)
        ]
        peak = scores[0]
        for s in scores[1:]:
            peak = jnp.maximum(peak, s)
        mass = jnp.zeros((2, 1), jnp.float32)
        mixed = jnp.zeros((2, HD), jnp.float32)
        for s, score in enumerate(scores):
            w = jnp.exp(score - peak)
            mass += w
            mixed += w * kvown[s, 2:4, :]
        return mixed / mass, peak + jnp.log(mass)

    def slot_state(i):
        rows = pl.ds(i * BLOCK, BLOCK)
        q = qall[owner_ref[i]]
        spot = lax.broadcasted_iota(jnp.int32, (8, 256), 1)
        line = lax.broadcasted_iota(jnp.int32, (8, 128), 0)
        q2 = jnp.concatenate(
            [jnp.where(line == j, q[j : j + 1], 0.0).astype(jnp.bfloat16) for j in (0, 1)], axis=1
        )
        scores = lax.dot_general(
            q2, kout[rows, :], (((1,), (1,)), ((), ())), preferred_element_type=jnp.float32
        )
        scores = jnp.where(spot < rows_ref[i], scores * scale, -1e30)
        peak = jnp.max(scores, axis=1, keepdims=True)
        w = jnp.exp(scores - peak)
        mass = jnp.sum(w, axis=1, keepdims=True)
        mixed = jnp.dot(w.astype(jnp.bfloat16), vout[rows, :], preferred_element_type=jnp.float32)
        mixed = mixed / mass
        lse = peak + jnp.log(mass)
        return jnp.where(sub2 == 0, mixed[0:2, :HD], mixed[0:2, HD:]), lse[0:2]

    def exchange_states(t):
        tag = []
        for i in range(3):
            mixed, lse = slot_state(i) if i < 2 else new_state(t)
            states[t, k, z, 2 * i : 2 * i + 2, :] = mixed
            tag += [lse[0:1], lse[1:2]]
        states[t, k, z, 6:7, :] = tag_row(tag)
        first, second = owner_ref[0].astype(jnp.float32), owner_ref[1].astype(jnp.float32)
        own = (k * 16 + z).astype(jnp.float32)
        states[t, k, z, 7:8, :] = tag_row([first, first, second, second, own, own, -1.0, -1.0])
        along_z(states.at[t, k, z], states.at[t, k, z], K_STATE + t)
        arrived(states.at[t, k, pl.ds(0, 15)], K_STATE + t)
        remote(states.at[t, k], states.at[t, k], K_STATEPAIR + t, sib)
        arrived(states.at[t, 1 - k], K_STATEPAIR + t)

    def attention(t, first, count):
        held = states[t].reshape(256, 128)
        total = [jnp.sum(states[t, core], axis=0) for core in (0, 1)]
        lse = jnp.concatenate([total[0][6:7], total[1][6:7]], axis=1)
        owner = jnp.concatenate([total[0][7:8], total[1][7:8]], axis=1)
        spot = lax.broadcasted_iota(jnp.int32, (count, 256), 1)
        conv = (lax.broadcasted_iota(jnp.int32, (count, 256), 0) + first).astype(jnp.float32)
        mine_ = owner == conv
        held = held.astype(jnp.bfloat16)
        parts = []
        for j in (0, 1):
            valid = mine_ & (lax.rem(spot, 2) == j)
            kept = jnp.where(valid, lse, -1e30)
            peak = jnp.max(kept, axis=1, keepdims=True)
            w = jnp.where(valid, jnp.exp(kept - peak), 0.0)
            w = w / jnp.sum(w, axis=1, keepdims=True)
            parts.append(
                jnp.dot(w.astype(jnp.bfloat16), held, preferred_element_type=jnp.float32)
            )
        return jnp.concatenate(parts, axis=1).astype(jnp.bfloat16)

    def plane(pick, dst, kind):
        def one(i, carry):
            dx, dy = 2 - i // NY, 2 - lax.rem(i, NY)
            to = hop(x, dx, NX) * NY + hop(y, dy, NY)

            @pl.when(to != me)
            def _():
                remote(pick(to), dst, kind, at(z, k, to // NY, lax.rem(to, NY)))

            return carry

        lax.fori_loop(0, NX * NY, one, 0)

    def next_tokens():
        half = attention(0, 16 * k, 16)
        for core in (0, 1):
            part = jnp.dot(half, wo2[core], preferred_element_type=jnp.float32).astype(jnp.bfloat16)
            osend[core] = part
            orecv[me, core] = part
        plane(lambda to: osend, orecv.at[me], K_OUT)
        arrived(orecv.at[pl.ds(0, 15)], K_OUT)
        tokens = []
        for core in (0, 1):
            out = jnp.sum(orecv[:, core].astype(jnp.float32), axis=0).astype(jnp.bfloat16)
            opair[k, core] = out
            tokens.append(
                (fresh_in[core, 1, k].astype(jnp.float32) + out.astype(jnp.float32)).astype(
                    jnp.bfloat16
                )
            )
        return tokens

    def own_columns(value, width, start):
        pick = lax.broadcasted_iota(jnp.int32, (16, width), 1) == (
            lax.broadcasted_iota(jnp.int32, (16, width), 0) + start
        )
        return lax.dot_general(
            pick.astype(jnp.bfloat16), value, (((1,), (1,)), ((), ())),
            preferred_element_type=jnp.float32,
        ).astype(jnp.bfloat16)

    def last_output():
        both = attention(1, 0, 32)
        part = jnp.dot(both, wo2[k], preferred_element_type=jnp.float32).astype(jnp.bfloat16)
        for side in (0, 1):
            fsend[side] = part[:, side * 128 : (side + 1) * 128]
        frecv[me] = fsend[me // 8]
        plane(lambda to: fsend.at[to // 8], frecv.at[me], K_LAST)
        out_ref[0] = own_columns(
            jnp.concatenate([opair[0, k], opair[1, k]], axis=0), 256, me * 16
        )
        arrived(frecv.at[pl.ds(0, 15)], K_LAST)
        out = jnp.sum(frecv[...].astype(jnp.float32), axis=0).astype(jnp.bfloat16)
        out_ref[1] = own_columns(out, 128, lax.rem(me, 8) * 16)

    for chunk in (0, 1):
        acc[chunk] = jnp.zeros(acc.shape[1:], jnp.float32)
    settled = -1
    done = -1
    for tick in range(NZ):
        if tick == 0:
            for chunk in (0, 1):
                for part in (0, 1):
                    for sign in (1, -1):
                        ring(0, chunk, part, zn[sign])
                hidden_slot(1 + chunk, False)
            hidden_slot(3, False)
            share_tick(0)
            pair_start()
        else:
            if tick == NZ - 1:
                settled += 1
                weight_settle(settled)
                products(done, tick - 1)
                done = tick - 1
            weight_slot(2 * tick - 1)
            if tick <= NZ // 2:
                hello()
            hidden_slot(tick, True)
            if tick + AHEAD < NZ:
                hidden_slot(tick + AHEAD, False)
            weight_slot(2 * tick)
            if tick <= NZ // 2:
                heard()
            share_tick(tick)
        if tick == 2:
            for copy in local:
                copy.wait()
            pair_finish()
            weight_settle(0)
            settled = 0
            project_first()
        if 3 <= tick <= NZ // 2:
            away = range(1, 4) if tick == 3 else (tick,)
            send_new(0, [dz for dz in Z_FAR_FIRST if abs(dz) in away])
        if tick == 11:
            query_first()
        if tick == 14:
            query_first_half()
        if tick in PRODUCT_TICKS:
            upto = tick - 1
            while settled < NZ // 2 and min(2 * (settled + 1), NZ - 1) <= upto:
                settled += 1
                weight_settle(settled)
            products(done, upto)
            done = upto
    last_products()
    query_first_rest()
    for slot in (0, 1):
        rows = pl.ds(slot * BLOCK, BLOCK)
        keep = lax.broadcasted_iota(jnp.int32, (BLOCK, BLOCK), 0) < rows_ref[slot]
        for chunk, out in ((0, kout), (1, vout)):
            out[rows, :] = jnp.where(keep, acc[chunk, rows, :], 0.0).astype(jnp.bfloat16)
    outs = [
        pltpu.make_async_copy(kout, key_ref, osem.at[0]),
        pltpu.make_async_copy(vout, value_ref, osem.at[1]),
    ]
    for copy in outs:
        copy.start()
    exchange_states(0)
    tokens = next_tokens()
    project_query(1, tokens)
    send_query(1)
    project_new(1, tokens)
    send_new(1)
    remote(opair.at[k, 1 - k], opair.at[k, 1 - k], K_OPAIR, sib)
    query_half(1)
    new_pair(1)
    departed(qall.at[pl.ds(0, 15)], K_Q)
    departed(qall.at[pl.ds(0, 16)], K_QPAIR)
    query_rest(1)
    exchange_states(1)
    arrived(opair.at[1 - k, k], K_OPAIR)
    last_output()

    pltpu.make_async_copy(hbuf.at[pl.ds(0, 15)], hbuf.at[pl.ds(0, 15)], hsend).wait()
    pltpu.make_async_copy(wbuf.at[pl.ds(0, 15)], wbuf.at[pl.ds(0, 15)], wsend).wait()
    pltpu.make_async_copy(wbuf.at[pl.ds(0, 16)], wbuf.at[pl.ds(0, 16)], sibsend).wait()
    departed(fresh_in.at[k], K_NEW)
    departed(wq2.at[k], K_WQ)
    departed(wo2.at[k], K_WO)
    departed(opair.at[k, 1 - k], K_OPAIR)
    departed(kvrecv.at[0, pl.ds(0, 15), pl.ds(0, 6)], K_KV)
    departed(qrecv.at[1, pl.ds(0, 15)], K_Q + 1)
    departed(kvrecv.at[1, pl.ds(0, 15), pl.ds(0, 4)], K_KV + 1)
    departed(qpair.at[1, k], K_QPAIR + 1)
    for t in (0, 1):
        departed(states.at[t, k, pl.ds(0, 15)], K_STATE + t)
        departed(states.at[t, k], K_STATEPAIR + t)
    departed(orecv.at[pl.ds(0, 15)], K_OUT)
    departed(frecv.at[pl.ds(0, 15)], K_LAST)
    for copy in outs:
        copy.wait()


def layer(hidden, slot_owner, slot_rows, new_hidden, w_query, w_key, w_value, w_out):
    rows, width = hidden.shape
    cols = w_key.shape[1]
    bf16, f32 = jnp.bfloat16, jnp.float32
    any_ = pl.BlockSpec(memory_space=pl.ANY)
    hbm = pl.BlockSpec(memory_space=pltpu.HBM)
    smem = pl.BlockSpec(memory_space=pltpu.SMEM)
    caches = [jax.ShapeDtypeStruct((rows, cols), bf16)] * 2
    dma = pltpu.SemaphoreType.DMA
    return pl.pallas_call(
        layer_kernel,
        out_shape=caches + [jax.ShapeDtypeStruct((STEPS, 16, 32), bf16)],
        in_specs=[smem, smem] + [hbm] * 6,
        out_specs=[any_, any_, pl.BlockSpec(memory_space=pltpu.VMEM)],
        scratch_shapes=[
            pltpu.VMEM((NX * NY, rows, width), bf16),
            pltpu.VMEM((2 * NZ, 2, BLOCK, cols), bf16),
            pltpu.VMEM((2, rows, cols), f32),
            pltpu.VMEM((rows, cols), bf16),
            pltpu.VMEM((rows, cols), bf16),
            pltpu.VMEM((2, STEPS, 2, 16, 256), bf16),
            pltpu.VMEM((2, 256, 256), bf16),
            pltpu.VMEM((2, 256, 256), bf16),
            pltpu.VMEM((STEPS, 16, 256), bf16),
            pltpu.VMEM((STEPS, NZ, 16, 256), bf16),
            pltpu.VMEM((STEPS, 2, 16, 256), bf16),
            pltpu.VMEM((32, 2, 128), f32),
            pltpu.VMEM((STEPS, NZ, 8, 128), f32),
            pltpu.VMEM((STEPS, NZ, 8, 128), f32),
            pltpu.VMEM((STEPS, 4, 128), f32),
            pltpu.VMEM((STEPS, 2, NZ, 8, 128), f32),
            pltpu.VMEM((2, 16, 256), bf16),
            pltpu.VMEM((16, 2, 16, 256), bf16),
            pltpu.VMEM((2, 2, 16, 256), bf16),
            pltpu.VMEM((2, 32, 128), bf16),
            pltpu.VMEM((16, 32, 128), bf16),
            dma, dma((NX * NY, 4)), dma, dma((2 * NZ, 2, 2)), dma, dma((6,)), dma((2,)),
            dma((KINDS,)), dma((KINDS,)), pltpu.SemaphoreType.REGULAR((2,)),
        ],
        compiler_params=pltpu.CompilerParams(
            collective_id=0, has_side_effects=True, vmem_limit_bytes=60 << 20
        ),
        name="layer",
    )(
        slot_owner, slot_rows, hidden, new_hidden.reshape(STEPS, 2, 16, 256),
        w_query, w_key, w_value, w_out,
    )


def solution(mesh):
    in_specs = (
        P("cache", "head"),
        P("cache"),
        P("cache"),
        P(None, None, "cache"),
        P("cache", "head"),
        P("cache", "head"),
        P("cache", "head"),
        P("head", "cache"),
    )
    out_specs = (P("cache", "head"), P("cache", "head"), P(None, None, ("cache", "head")))

    def on_device(*arrays):
        key, value, out = layer(*arrays)
        low, high = jnp.finfo(key.dtype).min, jnp.finfo(key.dtype).max
        return lax.clamp(low, key, high), lax.clamp(low, value, high), jnp.swapaxes(out, 1, 2)

    return jax.shard_map(
        on_device, mesh=mesh, in_specs=in_specs, out_specs=out_specs, check_vma=False
    )
```

```python
import jax
import jax.numpy as jnp
from jax import lax
from jax.experimental import pallas as pl
from jax.experimental.pallas import tpu as pltpu
from jax.sharding import PartitionSpec as P

HD = 128
STEPS = 2
MESH = pl.DeviceIdType.MESH
NX, NY, NZ = 4, 4, 16
BLOCK = 256
QUARTER = 128


def place():
    c = lax.axis_index("cache")
    h = lax.axis_index("head")
    return c // 2, lax.rem(c, 2), h // NY, lax.rem(h, NY)


def at(z, k, x, y):
    return {"cache": z * 2 + k, "head": x * NY + y}


def hop(value, by, size):
    return lax.rem(value + (by + size), size)
Z_FAR_FIRST = (8, 7, -7, 6, -6, 5, -5, 4, -4, 3, -3, 2, -2, 1, -1)
PLANE_FAR_FIRST = tuple(
    sorted(
        ((dx, dy) for dx in (2, 1, -1, 0) for dy in (2, 1, -1, 0) if dx or dy),
        key=lambda d: -abs(d[0]) - abs(d[1]),
    )
)
K_NEW, K_WQ, K_WO, K_OPAIR, K_OUT, K_LAST = range(6)
K_Q, K_KV, K_QPAIR, K_STATE, K_STATEPAIR = 6, 8, 10, 12, 14
KINDS = 16
PRODUCT_TICKS = (5, 7, 9, 11, 12, 13, 14)
AHEAD = 3


def layer_kernel(
    owner_ref, rows_ref, hidden_ref, new_ref, wq_ref, wk_ref, wv_ref, wo_ref,
    key_ref, value_ref, out_ref,
    hbuf, wbuf, acc, kout, vout, fresh_in, wq2, wo2,
    qsend, qrecv, qpair, qall, kvsend, kvrecv, kvown, states, osend, orecv, opair, fsend, frecv,
    hsend, hsem, wsend, wsem, sibsend, lsem, osem, msem, mrecv, hellos,
):
    z, k, x, y = place()
    me = x * NY + y
    mine = z * 2 + k
    xn = {s: at(z, k, hop(x, s, NX), y) for s in (1, -1)}
    yn = {s: at(z, k, x, hop(y, s, NY)) for s in (1, -1)}
    zn = {s: at(hop(z, s, NZ), k, x, y) for s in (1, -1)}
    sib = at(z, 1 - k, x, y)
    barrier = pltpu.get_barrier_semaphore()
    partners = [sib, xn[1], xn[-1], yn[1], yn[-1], zn[1], zn[-1]]
    for other in partners:
        pl.semaphore_signal(barrier, inc=1, device_id=other, device_id_type=MESH)
    local = [
        pltpu.make_async_copy(hidden_ref, hbuf.at[me], lsem.at[0]),
        pltpu.make_async_copy(wk_ref, wbuf.at[mine, 0], lsem.at[1]),
        pltpu.make_async_copy(wv_ref, wbuf.at[mine, 1], lsem.at[2]),
        pltpu.make_async_copy(new_ref, fresh_in.at[k], lsem.at[3]),
        pltpu.make_async_copy(wq_ref, wq2.at[k], lsem.at[4]),
        pltpu.make_async_copy(wo_ref, wo2.at[k], lsem.at[5]),
    ]
    for copy in local:
        copy.start()
    pl.semaphore_wait(barrier, len(partners))

    def source(dx, dy):
        return hop(x, dx, NX) * NY + hop(y, dy, NY)

    def push(dx, dy, piece, to, own=False):
        index = source(dx, dy)
        rows = pl.ds(piece * QUARTER, QUARTER)
        src = hidden_ref.at[rows] if own else hbuf.at[index, rows]
        pltpu.make_async_remote_copy(
            src_ref=src, dst_ref=hbuf.at[index, rows],
            send_sem=hsend, recv_sem=hsem.at[index, piece],
            device_id=to, device_id_type=MESH,
        ).start()

    def landed(dx, dy, pieces):
        index = source(dx, dy)
        for piece in pieces:
            part = hbuf.at[index, pl.ds(piece * QUARTER, QUARTER)]
            pltpu.make_async_copy(part, part, hsem.at[index, piece]).wait()

    def piece_of(half, sign, turn):
        return 2 * half + (turn if sign == 1 else 1 - turn)

    SLOTS = {
        1: ("own", 0, 0), 2: ("own", 0, 1), 3: ("own", 1, 0), 4: ("own", 1, 1), 5: ("pass", 0, 0),
        6: (-1, 1, 0), 7: (-1, 1, 1), 8: (1, 1, 0), 9: (1, 1, 1), 10: ("pass", 1, 0),
        11: (2, 1, 0), 12: (2, 1, 1), 13: ("pass", 1, -1), 14: ("pass", 1, 1), 15: ("pass", 1, 2),
    }

    def hidden_slot(slot, arriving):
        what, axis, turn = SLOTS[slot]
        for half in (0, 1):
            nb = xn if axis == half else yn
            for sign in (1, -1):
                if what == "pass":
                    a, b = (-sign, 0) if axis == 0 else (turn, -sign)
                    piece = piece_of(half, sign, 0)
                    if arriving:
                        a, b = (2, 0) if axis == 0 else (turn, 2)
                else:
                    a, b = (0, 0) if what == "own" else (what, 0)
                    piece = piece_of(half, sign, turn)
                    if arriving:
                        a, b = (-sign, b) if axis == 0 else (a, -sign)
                dx, dy = (a, b) if half == 0 else (b, a)
                if arriving:
                    landed(dx, dy, (piece,))
                else:
                    push(dx, dy, piece, nb[sign], own=what == "own")

    def ready(dx, dy):
        ax, ay = jnp.minimum(dx, NX - dx), jnp.minimum(dy, NY - dy)
        near = ax + ay
        side = jnp.where((dx == 3) | (dy == 3), 13, 14)
        both = jnp.where((dx == 3) & (dy == 3), 7, 9)
        straight = jnp.where(near == 1, 4, 10)
        far = jnp.where(near == 4, 15, side)
        out = jnp.where(near == 2, both, far)
        out = jnp.where((ax == 0) | (ay == 0), straight, out)
        return jnp.where(near == 0, 0, out)

    def block(dz, core):
        return hop(z, dz, NZ) * 2 + core

    def ring(dz, chunk, part, to):
        rows = pl.ds(part * QUARTER, QUARTER)
        held = wbuf.at[block(dz, k), chunk, rows]
        src = (wk_ref if chunk == 0 else wv_ref).at[rows] if dz == 0 else held
        pltpu.make_async_remote_copy(
            src_ref=src, dst_ref=held, send_sem=wsend,
            recv_sem=wsem.at[block(dz, k), chunk, part],
            device_id=to, device_id_type=MESH,
        ).start()

    def share(dz, chunk, part=None):
        held, sem = wbuf.at[block(dz, k), chunk], wsem.at[block(dz, k), chunk, part or 0]
        src = (wk_ref if chunk == 0 else wv_ref) if dz == 0 else held
        if part is not None:
            held = held.at[pl.ds(part * QUARTER, QUARTER)]
            src = held
        pltpu.make_async_remote_copy(
            src_ref=src, dst_ref=held, send_sem=sibsend, recv_sem=sem,
            device_id=sib, device_id_type=MESH,
        ).start()

    def have(dz, core, chunk):
        part = wbuf.at[block(dz, core), chunk]
        pltpu.make_async_copy(part, part, wsem.at[block(dz, core), chunk, 0]).wait()

    def have_part(dz, chunk, part, core=k):
        held = wbuf.at[block(dz, core), chunk, pl.ds(part * QUARTER, QUARTER)]
        pltpu.make_async_copy(held, held, wsem.at[block(dz, core), chunk, part]).wait()

    def weight_slot(slot):
        r, chunk, part = (slot + 3) // 4, (slot - 1) % 4 // 2, (slot - 1) % 2
        if r < NZ // 2:
            for sign in (1, -1):
                have_part(-sign * r, chunk, part)
                if r < NZ // 2 - 1 or (sign == 1) == (chunk == 0):
                    ring(-sign * r, chunk, part, zn[sign])
        else:
            for chunk in (0, 1):
                have_part(NZ // 2, chunk, part)
                share(NZ // 2, chunk, part)

    def hello():
        for side, sign in ((0, 1), (1, -1)):
            pl.semaphore_signal(hellos.at[side], inc=1, device_id=zn[sign], device_id_type=MESH)

    def heard():
        for side in (0, 1):
            pl.semaphore_wait(hellos.at[side], 1)

    def share_tick(tick):
        if tick == 0:
            for chunk in (0, 1):
                share(0, chunk)
        elif tick < NZ - 1:
            for sign in (1, -1):
                share(-sign * ((tick + 1) // 2), (tick + 1) % 2)

    def weight_settle(r):
        for dz in ((r, -r) if 0 < r < NZ // 2 else (r,)):
            for chunk in (0, 1):
                have(dz, 1 - k, chunk)

    def add(h, cores):
        for chunk in (0, 1):
            part = None
            for core in cores:
                term = jnp.dot(
                    hbuf[h, :, pl.ds(pl.multiple_of(core * BLOCK, BLOCK), BLOCK)], wbuf[2 * h + core, chunk],
                    preferred_element_type=jnp.float32,
                )
                part = term if part is None else part + term
            acc[chunk] += part

    def last_products():
        corner, across = source(2, 2), hop(z, NZ // 2, NZ)

        @pl.when(corner != across)
        def _():
            add(corner, (0, 1))

        add(across, (k,))
        for part in (0, 1):
            for chunk in (0, 1):
                have_part(NZ // 2, chunk, part, 1 - k)
        add(across, (1 - k,))

    def products(after, upto):
        def one(h, carry):
            due = ready(hop(h // NY, NX - x, NX), hop(lax.rem(h, NY), NY - y, NY))
            away = hop(h, NZ - z, NZ)
            due = jnp.maximum(due, jnp.minimum(2 * jnp.minimum(away, NZ - away), NZ - 1))
            now = (due > after) & (due <= upto)

            @pl.when(now)
            def _():
                add(h, (0, 1))

            return carry

        lax.fori_loop(0, NX * NY, one, 0)

    def remote(src, dst, kind, to):
        pltpu.make_async_remote_copy(
            src_ref=src, dst_ref=dst, send_sem=msem.at[kind], recv_sem=mrecv.at[kind],
            device_id=to, device_id_type=MESH,
        ).start()

    def arrived(part, kind):
        pltpu.make_async_copy(part, part, mrecv.at[kind]).wait()

    def departed(part, kind):
        pltpu.make_async_copy(part, part, msem.at[kind]).wait()

    def each_z(send):
        def one(i, carry):
            d = NZ // 2 - (i + 1) // 2
            send(hop(z, jnp.where(lax.rem(i, 2) == 1, d, -d), NZ))
            return carry

        lax.fori_loop(0, NZ - 1, one, 0)

    def along_z(src, dst, kind):
        each_z(lambda to: remote(src, dst, kind, at(to, k, x, y)))

    lane = lax.broadcasted_iota(jnp.int32, (1, 128), 1)

    def tag_row(values):
        row = jnp.zeros((1, 128), jnp.float32)
        for r, value in enumerate(values):
            row = jnp.where(lane == z * 8 + r, value, row)
        return row

    def pair_start():
        remote(new_ref, fresh_in.at[k], K_NEW, sib)
        remote(wq_ref, wq2.at[k], K_WQ, sib)
        remote(wo_ref, wo2.at[k], K_WO, sib)

    def pair_finish():
        arrived(fresh_in.at[k], K_NEW)
        arrived(wq2.at[k], K_WQ)
        arrived(wo2.at[k], K_WO)

    def project_query(t, tokens):
        q = jnp.zeros((16, 256), jnp.float32)
        for core in (0, 1):
            q += jnp.dot(tokens[core], wq2[core], preferred_element_type=jnp.float32)
        q16 = q.astype(jnp.bfloat16)
        qsend[t] = q16
        qrecv[t, z] = q16

    def send_query(t):
        along_z(qsend.at[t], qrecv.at[t, z], K_Q + t)

    def project_new(t, tokens):
        for chunk in (0, 1):
            kv = jnp.zeros((16, 256), jnp.float32)
            for core in (0, 1):
                kv += jnp.dot(
                    tokens[core], wbuf[2 * z + core, chunk], preferred_element_type=jnp.float32
                )
            for j in (0, 1):
                kvsend[t, :, 2 * chunk + j, :] = kv[:, j * HD : (j + 1) * HD]

    def send_new(t, offsets=None):
        rows = pl.ds(0, 6 if t == 0 else 4)

        def send(to):
            remote(kvsend.at[t, to, rows], kvrecv.at[t, z, rows], K_KV + t, at(to, k, x, y))

        if offsets is None:
            each_z(send)
        else:
            for dz in offsets:
                send(hop(z, dz, NZ))

    def project_first():
        tokens = [fresh_in[0, 0, k], fresh_in[1, 0, k]]
        project_new(0, tokens)
        q = jnp.zeros((16, 256), jnp.float32)
        for core in (0, 1):
            q += jnp.dot(tokens[core], wq2[core], preferred_element_type=jnp.float32)
        for j in (0, 1):
            kvsend[0, :, 4 + j, :] = q[:, j * HD : (j + 1) * HD]

    def query_first():
        new_pair(0)
        along_z(qall.at[k * 16 + z], qall.at[k * 16 + z], K_Q)

    def query_first_half():
        arrived(qall.at[pl.ds(0, 15)], K_Q)
        half = qall.at[pl.ds(k * 16, 16)]
        remote(half, half, K_QPAIR, sib)

    def query_first_rest():
        arrived(qall.at[pl.ds(0, 16)], K_QPAIR)

    def query_half(t):
        arrived(qrecv.at[t, pl.ds(0, 15)], K_Q + t)
        half = jnp.sum(qrecv[t].astype(jnp.float32), axis=0).astype(jnp.bfloat16)
        qpair[t, k] = half
        remote(qpair.at[t, k], qpair.at[t, k], K_QPAIR + t, sib)
        return half.astype(jnp.float32)

    def query_rest(t):
        arrived(qpair.at[t, 1 - k], K_QPAIR + t)
        for half in (0, 1):
            q = qpair[t, half].astype(jnp.float32)
            for j in (0, 1):
                qall[16 * half : 16 * half + 16, j, :] = q[:, j * HD : (j + 1) * HD]

    def new_pair(t):
        rows = 6 if t == 0 else 4
        kvrecv[t, z] = kvsend[t, z]
        arrived(kvrecv.at[t, pl.ds(0, 15), pl.ds(0, rows)], K_KV + t)
        total = jnp.sum(kvrecv[t, :, 0:rows, :], axis=0).astype(jnp.bfloat16).astype(jnp.float32)
        kvown[t] = total[0:4]
        if t == 0:
            qall[k * 16 + z] = total[4:6]

    scale = HD ** (-0.5)
    sub2 = lax.broadcasted_iota(jnp.int32, (2, 128), 0)

    def new_state(t):
        q2 = qall[k * 16 + z]
        scores = [
            jnp.sum(q2 * kvown[s, 0:2, :], axis=1, keepdims=True) * scale for s in range(t + 1)
        ]
        peak = scores[0]
        for s in scores[1:]:
            peak = jnp.maximum(peak, s)
        mass = jnp.zeros((2, 1), jnp.float32)
        mixed = jnp.zeros((2, HD), jnp.float32)
        for s, score in enumerate(scores):
            w = jnp.exp(score - peak)
            mass += w
            mixed += w * kvown[s, 2:4, :]
        return mixed / mass, peak + jnp.log(mass)

    def slot_state(i):
        rows = pl.ds(i * BLOCK, BLOCK)
        q = qall[owner_ref[i]]
        spot = lax.broadcasted_iota(jnp.int32, (8, 256), 1)
        line = lax.broadcasted_iota(jnp.int32, (8, 128), 0)
        q2 = jnp.concatenate(
            [jnp.where(line == j, q[j : j + 1], 0.0).astype(jnp.bfloat16) for j in (0, 1)], axis=1
        )
        scores = lax.dot_general(
            q2, kout[rows, :], (((1,), (1,)), ((), ())), preferred_element_type=jnp.float32
        )
        scores = jnp.where(spot < rows_ref[i], scores * scale, -1e30)
        peak = jnp.max(scores, axis=1, keepdims=True)
        w = jnp.exp(scores - peak)
        mass = jnp.sum(w, axis=1, keepdims=True)
        mixed = jnp.dot(w.astype(jnp.bfloat16), vout[rows, :], preferred_element_type=jnp.float32)
        mixed = mixed / mass
        lse = peak + jnp.log(mass)
        return jnp.where(sub2 == 0, mixed[0:2, :HD], mixed[0:2, HD:]), lse[0:2]

    def exchange_states(t):
        tag = []
        for i in range(3):
            mixed, lse = slot_state(i) if i < 2 else new_state(t)
            states[t, k, z, 2 * i : 2 * i + 2, :] = mixed
            tag += [lse[0:1], lse[1:2]]
        states[t, k, z, 6:7, :] = tag_row(tag)
        first, second = owner_ref[0].astype(jnp.float32), owner_ref[1].astype(jnp.float32)
        own = (k * 16 + z).astype(jnp.float32)
        states[t, k, z, 7:8, :] = tag_row([first, first, second, second, own, own, -1.0, -1.0])
        along_z(states.at[t, k, z], states.at[t, k, z], K_STATE + t)
        arrived(states.at[t, k, pl.ds(0, 15)], K_STATE + t)
        remote(states.at[t, k], states.at[t, k], K_STATEPAIR + t, sib)
        arrived(states.at[t, 1 - k], K_STATEPAIR + t)

    def attention(t, first, count):
        held = states[t].reshape(256, 128)
        total = [jnp.sum(states[t, core], axis=0) for core in (0, 1)]
        lse = jnp.concatenate([total[0][6:7], total[1][6:7]], axis=1)
        owner = jnp.concatenate([total[0][7:8], total[1][7:8]], axis=1)
        spot = lax.broadcasted_iota(jnp.int32, (count, 256), 1)
        conv = (lax.broadcasted_iota(jnp.int32, (count, 256), 0) + first).astype(jnp.float32)
        mine_ = owner == conv
        held = held.astype(jnp.bfloat16)
        parts = []
        for j in (0, 1):
            valid = mine_ & (lax.rem(spot, 2) == j)
            kept = jnp.where(valid, lse, -1e30)
            peak = jnp.max(kept, axis=1, keepdims=True)
            w = jnp.where(valid, jnp.exp(kept - peak), 0.0)
            w = w / jnp.sum(w, axis=1, keepdims=True)
            parts.append(
                jnp.dot(w.astype(jnp.bfloat16), held, preferred_element_type=jnp.float32)
            )
        return jnp.concatenate(parts, axis=1).astype(jnp.bfloat16)

    def plane(pick, dst, kind):
        def one(i, carry):
            dx, dy = 2 - i // NY, 2 - lax.rem(i, NY)
            to = hop(x, dx, NX) * NY + hop(y, dy, NY)

            @pl.when(to != me)
            def _():
                remote(pick(to), dst, kind, at(z, k, to // NY, lax.rem(to, NY)))

            return carry

        lax.fori_loop(0, NX * NY, one, 0)

    def next_tokens():
        half = attention(0, 16 * k, 16)
        for core in (0, 1):
            part = jnp.dot(half, wo2[core], preferred_element_type=jnp.float32).astype(jnp.bfloat16)
            osend[core] = part
            orecv[me, core] = part
        plane(lambda to: osend, orecv.at[me], K_OUT)
        arrived(orecv.at[pl.ds(0, 15)], K_OUT)
        tokens = []
        for core in (0, 1):
            out = jnp.sum(orecv[:, core].astype(jnp.float32), axis=0).astype(jnp.bfloat16)
            opair[k, core] = out
            tokens.append(
                (fresh_in[core, 1, k].astype(jnp.float32) + out.astype(jnp.float32)).astype(
                    jnp.bfloat16
                )
            )
        return tokens

    def own_columns(value, width, start):
        pick = lax.broadcasted_iota(jnp.int32, (16, width), 1) == (
            lax.broadcasted_iota(jnp.int32, (16, width), 0) + start
        )
        return lax.dot_general(
            pick.astype(jnp.bfloat16), value, (((1,), (1,)), ((), ())),
            preferred_element_type=jnp.float32,
        ).astype(jnp.bfloat16)

    def last_output():
        both = attention(1, 0, 32)
        part = jnp.dot(both, wo2[k], preferred_element_type=jnp.float32).astype(jnp.bfloat16)
        for side in (0, 1):
            fsend[side] = part[:, side * 128 : (side + 1) * 128]
        frecv[me] = fsend[me // 8]
        plane(lambda to: fsend.at[to // 8], frecv.at[me], K_LAST)
        out_ref[0] = own_columns(
            jnp.concatenate([opair[0, k], opair[1, k]], axis=0), 256, me * 16
        )
        arrived(frecv.at[pl.ds(0, 15)], K_LAST)
        out = jnp.sum(frecv[...].astype(jnp.float32), axis=0).astype(jnp.bfloat16)
        out_ref[1] = own_columns(out, 128, lax.rem(me, 8) * 16)

    for chunk in (0, 1):
        acc[chunk] = jnp.zeros(acc.shape[1:], jnp.float32)
    settled = -1
    done = -1
    for tick in range(NZ):
        if tick == 0:
            for chunk in (0, 1):
                for part in (0, 1):
                    for sign in (1, -1):
                        ring(0, chunk, part, zn[sign])
                hidden_slot(1 + chunk, False)
            hidden_slot(3, False)
            share_tick(0)
            pair_start()
        else:
            if tick == NZ - 1:
                settled += 1
                weight_settle(settled)
                products(done, tick - 1)
                done = tick - 1
            weight_slot(2 * tick - 1)
            if tick <= NZ // 2:
                hello()
            hidden_slot(tick, True)
            if tick + AHEAD < NZ:
                hidden_slot(tick + AHEAD, False)
            weight_slot(2 * tick)
            if tick <= NZ // 2:
                heard()
            share_tick(tick)
        if tick == 2:
            for copy in local:
                copy.wait()
            pair_finish()
            weight_settle(0)
            settled = 0
            project_first()
        if 3 <= tick <= NZ // 2:
            away = range(1, 4) if tick == 3 else (tick,)
            send_new(0, [dz for dz in Z_FAR_FIRST if abs(dz) in away])
        if tick == 11:
            query_first()
        if tick == 14:
            query_first_half()
        if tick in PRODUCT_TICKS:
            upto = tick - 1
            while settled < NZ // 2 and min(2 * (settled + 1), NZ - 1) <= upto:
                settled += 1
                weight_settle(settled)
            products(done, upto)
            done = upto
    last_products()
    query_first_rest()
    for slot in (0, 1):
        rows = pl.ds(slot * BLOCK, BLOCK)
        keep = lax.broadcasted_iota(jnp.int32, (BLOCK, BLOCK), 0) < rows_ref[slot]
        for chunk, out in ((0, kout), (1, vout)):
            out[rows, :] = jnp.where(keep, acc[chunk, rows, :], 0.0).astype(jnp.bfloat16)
    outs = [
        pltpu.make_async_copy(kout, key_ref, osem.at[0]),
        pltpu.make_async_copy(vout, value_ref, osem.at[1]),
    ]
    for copy in outs:
        copy.start()
    exchange_states(0)
    tokens = next_tokens()
    project_query(1, tokens)
    send_query(1)
    project_new(1, tokens)
    send_new(1)
    remote(opair.at[k, 1 - k], opair.at[k, 1 - k], K_OPAIR, sib)
    query_half(1)
    new_pair(1)
    departed(qall.at[pl.ds(0, 15)], K_Q)
    departed(qall.at[pl.ds(0, 16)], K_QPAIR)
    query_rest(1)
    exchange_states(1)
    arrived(opair.at[1 - k, k], K_OPAIR)
    last_output()

    pltpu.make_async_copy(hbuf.at[pl.ds(0, 15)], hbuf.at[pl.ds(0, 15)], hsend).wait()
    pltpu.make_async_copy(wbuf.at[pl.ds(0, 15)], wbuf.at[pl.ds(0, 15)], wsend).wait()
    pltpu.make_async_copy(wbuf.at[pl.ds(0, 16)], wbuf.at[pl.ds(0, 16)], sibsend).wait()
    departed(fresh_in.at[k], K_NEW)
    departed(wq2.at[k], K_WQ)
    departed(wo2.at[k], K_WO)
    departed(opair.at[k, 1 - k], K_OPAIR)
    departed(kvrecv.at[0, pl.ds(0, 15), pl.ds(0, 6)], K_KV)
    departed(qrecv.at[1, pl.ds(0, 15)], K_Q + 1)
    departed(kvrecv.at[1, pl.ds(0, 15), pl.ds(0, 4)], K_KV + 1)
    departed(qpair.at[1, k], K_QPAIR + 1)
    for t in (0, 1):
        departed(states.at[t, k, pl.ds(0, 15)], K_STATE + t)
        departed(states.at[t, k], K_STATEPAIR + t)
    departed(orecv.at[pl.ds(0, 15)], K_OUT)
    departed(frecv.at[pl.ds(0, 15)], K_LAST)
    for copy in outs:
        copy.wait()


def layer(hidden, slot_owner, slot_rows, new_hidden, w_query, w_key, w_value, w_out):
    rows, width = hidden.shape
    cols = w_key.shape[1]
    bf16, f32 = jnp.bfloat16, jnp.float32
    any_ = pl.BlockSpec(memory_space=pl.ANY)
    hbm = pl.BlockSpec(memory_space=pltpu.HBM)
    smem = pl.BlockSpec(memory_space=pltpu.SMEM)
    caches = [jax.ShapeDtypeStruct((rows, cols), bf16)] * 2
    dma = pltpu.SemaphoreType.DMA
    return pl.pallas_call(
        layer_kernel,
        out_shape=caches + [jax.ShapeDtypeStruct((STEPS, 16, 32), bf16)],
        in_specs=[smem, smem] + [hbm] * 6,
        out_specs=[any_, any_, pl.BlockSpec(memory_space=pltpu.VMEM)],
        scratch_shapes=[
            pltpu.VMEM((NX * NY, rows, width), bf16),
            pltpu.VMEM((2 * NZ, 2, BLOCK, cols), bf16),
            pltpu.VMEM((2, rows, cols), f32),
            pltpu.VMEM((rows, cols), bf16),
            pltpu.VMEM((rows, cols), bf16),
            pltpu.VMEM((2, STEPS, 2, 16, 256), bf16),
            pltpu.VMEM((2, 256, 256), bf16),
            pltpu.VMEM((2, 256, 256), bf16),
            pltpu.VMEM((STEPS, 16, 256), bf16),
            pltpu.VMEM((STEPS, NZ, 16, 256), bf16),
            pltpu.VMEM((STEPS, 2, 16, 256), bf16),
            pltpu.VMEM((32, 2, 128), f32),
            pltpu.VMEM((STEPS, NZ, 8, 128), f32),
            pltpu.VMEM((STEPS, NZ, 8, 128), f32),
            pltpu.VMEM((STEPS, 4, 128), f32),
            pltpu.VMEM((STEPS, 2, NZ, 8, 128), f32),
            pltpu.VMEM((2, 16, 256), bf16),
            pltpu.VMEM((16, 2, 16, 256), bf16),
            pltpu.VMEM((2, 2, 16, 256), bf16),
            pltpu.VMEM((2, 32, 128), bf16),
            pltpu.VMEM((16, 32, 128), bf16),
            dma, dma((NX * NY, 4)), dma, dma((2 * NZ, 2, 2)), dma, dma((6,)), dma((2,)),
            dma((KINDS,)), dma((KINDS,)), pltpu.SemaphoreType.REGULAR((2,)),
        ],
        compiler_params=pltpu.CompilerParams(
            collective_id=0, has_side_effects=True, vmem_limit_bytes=60 << 20
        ),
        name="layer",
    )(
        slot_owner, slot_rows, hidden, new_hidden.reshape(STEPS, 2, 16, 256),
        w_query, w_key, w_value, w_out,
    )


def solution(mesh):
    in_specs = (
        P("cache", "head"),
        P("cache"),
        P("cache"),
        P(None, None, "cache"),
        P("cache", "head"),
        P("cache", "head"),
        P("cache", "head"),
        P("head", "cache"),
    )
    out_specs = (P("cache", "head"), P("cache", "head"), P(None, None, ("cache", "head")))

    def on_device(*arrays):
        key, value, out = layer(*arrays)
        low, high = jnp.finfo(key.dtype).min, jnp.finfo(key.dtype).max
        return lax.clamp(low, key, high), lax.clamp(low, value, high), jnp.swapaxes(out, 1, 2)

    return jax.shard_map(
        on_device, mesh=mesh, in_specs=in_specs, out_specs=out_specs, check_vma=False
    )
```

```python
import jax
import jax.numpy as jnp
from jax import lax
from jax.experimental import pallas as pl
from jax.experimental.pallas import tpu as pltpu
from jax.sharding import PartitionSpec as P

HD = 128
STEPS = 2
MESH = pl.DeviceIdType.MESH
NX, NY, NZ = 4, 4, 16
BLOCK = 256
QUARTER = 128


def place():
    c = lax.axis_index("cache")
    h = lax.axis_index("head")
    return c // 2, lax.rem(c, 2), h // NY, lax.rem(h, NY)


def at(z, k, x, y):
    return {"cache": z * 2 + k, "head": x * NY + y}


def hop(value, by, size):
    return lax.rem(value + (by + size), size)
Z_FAR_FIRST = (8, 7, -7, 6, -6, 5, -5, 4, -4, 3, -3, 2, -2, 1, -1)
PLANE_FAR_FIRST = tuple(
    sorted(
        ((dx, dy) for dx in (2, 1, -1, 0) for dy in (2, 1, -1, 0) if dx or dy),
        key=lambda d: -abs(d[0]) - abs(d[1]),
    )
)
K_NEW, K_WQ, K_WO, K_OPAIR, K_OUT, K_LAST = range(6)
K_Q, K_KV, K_QPAIR, K_STATE, K_STATEPAIR = 6, 8, 10, 12, 14
KINDS = 16
PRODUCT_TICKS = (5, 7, 9, 11, 12, 13, 14)
AHEAD = 3


def layer_kernel(
    owner_ref, rows_ref, hidden_ref, new_ref, wq_ref, wk_ref, wv_ref, wo_ref,
    key_ref, value_ref, out_ref,
    hbuf, wbuf, acc, kout, vout, fresh_in, wq2, wo2,
    qsend, qrecv, qpair, qall, kvsend, kvrecv, kvown, states, osend, orecv, opair, fsend, frecv,
    hsend, hsem, wsend, wsem, sibsend, lsem, osem, msem, mrecv, hellos,
):
    z, k, x, y = place()
    me = x * NY + y
    mine = z * 2 + k
    xn = {s: at(z, k, hop(x, s, NX), y) for s in (1, -1)}
    yn = {s: at(z, k, x, hop(y, s, NY)) for s in (1, -1)}
    zn = {s: at(hop(z, s, NZ), k, x, y) for s in (1, -1)}
    sib = at(z, 1 - k, x, y)
    barrier = pltpu.get_barrier_semaphore()
    partners = [sib, xn[1], xn[-1], yn[1], yn[-1], zn[1], zn[-1]]
    for other in partners:
        pl.semaphore_signal(barrier, inc=1, device_id=other, device_id_type=MESH)
    local = [
        pltpu.make_async_copy(hidden_ref, hbuf.at[me], lsem.at[0]),
        pltpu.make_async_copy(wk_ref, wbuf.at[mine, 0], lsem.at[1]),
        pltpu.make_async_copy(wv_ref, wbuf.at[mine, 1], lsem.at[2]),
        pltpu.make_async_copy(new_ref, fresh_in.at[k], lsem.at[3]),
        pltpu.make_async_copy(wq_ref, wq2.at[k], lsem.at[4]),
        pltpu.make_async_copy(wo_ref, wo2.at[k], lsem.at[5]),
    ]
    for copy in local:
        copy.start()
    pl.semaphore_wait(barrier, len(partners))

    def source(dx, dy):
        return hop(x, dx, NX) * NY + hop(y, dy, NY)

    def push(dx, dy, piece, to, own=False):
        index = source(dx, dy)
        rows = pl.ds(piece * QUARTER, QUARTER)
        src = hidden_ref.at[rows] if own else hbuf.at[index, rows]
        pltpu.make_async_remote_copy(
            src_ref=src, dst_ref=hbuf.at[index, rows],
            send_sem=hsend, recv_sem=hsem.at[index, piece],
            device_id=to, device_id_type=MESH,
        ).start()

    def landed(dx, dy, pieces):
        index = source(dx, dy)
        for piece in pieces:
            part = hbuf.at[index, pl.ds(piece * QUARTER, QUARTER)]
            pltpu.make_async_copy(part, part, hsem.at[index, piece]).wait()

    def piece_of(half, sign, turn):
        return 2 * half + (turn if sign == 1 else 1 - turn)

    SLOTS = {
        1: ("own", 0, 0), 2: ("own", 0, 1), 3: ("own", 1, 0), 4: ("own", 1, 1), 5: ("pass", 0, 0),
        6: (-1, 1, 0), 7: (-1, 1, 1), 8: (1, 1, 0), 9: (1, 1, 1), 10: ("pass", 1, 0),
        11: (2, 1, 0), 12: (2, 1, 1), 13: ("pass", 1, -1), 14: ("pass", 1, 1), 15: ("pass", 1, 2),
    }

    def hidden_slot(slot, arriving):
        what, axis, turn = SLOTS[slot]
        for half in (0, 1):
            nb = xn if axis == half else yn
            for sign in (1, -1):
                if what == "pass":
                    a, b = (-sign, 0) if axis == 0 else (turn, -sign)
                    piece = piece_of(half, sign, 0)
                    if arriving:
                        a, b = (2, 0) if axis == 0 else (turn, 2)
                else:
                    a, b = (0, 0) if what == "own" else (what, 0)
                    piece = piece_of(half, sign, turn)
                    if arriving:
                        a, b = (-sign, b) if axis == 0 else (a, -sign)
                dx, dy = (a, b) if half == 0 else (b, a)
                if arriving:
                    landed(dx, dy, (piece,))
                else:
                    push(dx, dy, piece, nb[sign], own=what == "own")

    def ready(dx, dy):
        ax, ay = jnp.minimum(dx, NX - dx), jnp.minimum(dy, NY - dy)
        near = ax + ay
        side = jnp.where((dx == 3) | (dy == 3), 13, 14)
        both = jnp.where((dx == 3) & (dy == 3), 7, 9)
        straight = jnp.where(near == 1, 4, 10)
        far = jnp.where(near == 4, 15, side)
        out = jnp.where(near == 2, both, far)
        out = jnp.where((ax == 0) | (ay == 0), straight, out)
        return jnp.where(near == 0, 0, out)

    def block(dz, core):
        return hop(z, dz, NZ) * 2 + core

    def ring(dz, chunk, part, to):
        rows = pl.ds(part * QUARTER, QUARTER)
        held = wbuf.at[block(dz, k), chunk, rows]
        src = (wk_ref if chunk == 0 else wv_ref).at[rows] if dz == 0 else held
        pltpu.make_async_remote_copy(
            src_ref=src, dst_ref=held, send_sem=wsend,
            recv_sem=wsem.at[block(dz, k), chunk, part],
            device_id=to, device_id_type=MESH,
        ).start()

    def share(dz, chunk, part=None):
        held, sem = wbuf.at[block(dz, k), chunk], wsem.at[block(dz, k), chunk, part or 0]
        src = (wk_ref if chunk == 0 else wv_ref) if dz == 0 else held
        if part is not None:
            held = held.at[pl.ds(part * QUARTER, QUARTER)]
            src = held
        pltpu.make_async_remote_copy(
            src_ref=src, dst_ref=held, send_sem=sibsend, recv_sem=sem,
            device_id=sib, device_id_type=MESH,
        ).start()

    def have(dz, core, chunk):
        part = wbuf.at[block(dz, core), chunk]
        pltpu.make_async_copy(part, part, wsem.at[block(dz, core), chunk, 0]).wait()

    def have_part(dz, chunk, part, core=k):
        held = wbuf.at[block(dz, core), chunk, pl.ds(part * QUARTER, QUARTER)]
        pltpu.make_async_copy(held, held, wsem.at[block(dz, core), chunk, part]).wait()

    def weight_slot(slot):
        r, chunk, part = (slot + 3) // 4, (slot - 1) % 4 // 2, (slot - 1) % 2
        if r < NZ // 2:
            for sign in (1, -1):
                have_part(-sign * r, chunk, part)
                if r < NZ // 2 - 1 or (sign == 1) == (chunk == 0):
                    ring(-sign * r, chunk, part, zn[sign])
        else:
            for chunk in (0, 1):
                have_part(NZ // 2, chunk, part)
                share(NZ // 2, chunk, part)

    def hello():
        for side, sign in ((0, 1), (1, -1)):
            pl.semaphore_signal(hellos.at[side], inc=1, device_id=zn[sign], device_id_type=MESH)

    def heard():
        for side in (0, 1):
            pl.semaphore_wait(hellos.at[side], 1)

    def share_tick(tick):
        if tick == 0:
            for chunk in (0, 1):
                share(0, chunk)
        elif tick < NZ - 1:
            for sign in (1, -1):
                share(-sign * ((tick + 1) // 2), (tick + 1) % 2)

    def weight_settle(r):
        for dz in ((r, -r) if 0 < r < NZ // 2 else (r,)):
            for chunk in (0, 1):
                have(dz, 1 - k, chunk)

    def add(h, cores):
        for chunk in (0, 1):
            part = None
            for core in cores:
                term = jnp.dot(
                    hbuf[h, :, pl.ds(pl.multiple_of(core * BLOCK, BLOCK), BLOCK)], wbuf[2 * h + core, chunk],
                    preferred_element_type=jnp.float32,
                )
                part = term if part is None else part + term
            acc[chunk] += part

    def last_products():
        corner, across = source(2, 2), hop(z, NZ // 2, NZ)

        @pl.when(corner != across)
        def _():
            add(corner, (0, 1))

        add(across, (k,))
        for part in (0, 1):
            for chunk in (0, 1):
                have_part(NZ // 2, chunk, part, 1 - k)
        add(across, (1 - k,))

    def products(after, upto):
        def one(h, carry):
            due = ready(hop(h // NY, NX - x, NX), hop(lax.rem(h, NY), NY - y, NY))
            away = hop(h, NZ - z, NZ)
            due = jnp.maximum(due, jnp.minimum(2 * jnp.minimum(away, NZ - away), NZ - 1))
            now = (due > after) & (due <= upto)

            @pl.when(now)
            def _():
                add(h, (0, 1))

            return carry

        lax.fori_loop(0, NX * NY, one, 0)

    def remote(src, dst, kind, to):
        pltpu.make_async_remote_copy(
            src_ref=src, dst_ref=dst, send_sem=msem.at[kind], recv_sem=mrecv.at[kind],
            device_id=to, device_id_type=MESH,
        ).start()

    def arrived(part, kind):
        pltpu.make_async_copy(part, part, mrecv.at[kind]).wait()

    def departed(part, kind):
        pltpu.make_async_copy(part, part, msem.at[kind]).wait()

    def each_z(send):
        def one(i, carry):
            d = NZ // 2 - (i + 1) // 2
            send(hop(z, jnp.where(lax.rem(i, 2) == 1, d, -d), NZ))
            return carry

        lax.fori_loop(0, NZ - 1, one, 0)

    def along_z(src, dst, kind):
        each_z(lambda to: remote(src, dst, kind, at(to, k, x, y)))

    lane = lax.broadcasted_iota(jnp.int32, (1, 128), 1)

    def tag_row(values):
        row = jnp.zeros((1, 128), jnp.float32)
        for r, value in enumerate(values):
            row = jnp.where(lane == z * 8 + r, value, row)
        return row

    def pair_start():
        remote(new_ref, fresh_in.at[k], K_NEW, sib)
        remote(wq_ref, wq2.at[k], K_WQ, sib)
        remote(wo_ref, wo2.at[k], K_WO, sib)

    def pair_finish():
        arrived(fresh_in.at[k], K_NEW)
        arrived(wq2.at[k], K_WQ)
        arrived(wo2.at[k], K_WO)

    def project_query(t, tokens):
        q = jnp.zeros((16, 256), jnp.float32)
        for core in (0, 1):
            q += jnp.dot(tokens[core], wq2[core], preferred_element_type=jnp.float32)
        q16 = q.astype(jnp.bfloat16)
        qsend[t] = q16
        qrecv[t, z] = q16

    def send_query(t):
        along_z(qsend.at[t], qrecv.at[t, z], K_Q + t)

    def project_new(t, tokens):
        for chunk in (0, 1):
            kv = jnp.zeros((16, 256), jnp.float32)
            for core in (0, 1):
                kv += jnp.dot(
                    tokens[core], wbuf[2 * z + core, chunk], preferred_element_type=jnp.float32
                )
            for j in (0, 1):
                kvsend[t, :, 2 * chunk + j, :] = kv[:, j * HD : (j + 1) * HD]

    def send_new(t, offsets=None):
        rows = pl.ds(0, 6 if t == 0 else 4)

        def send(to):
            remote(kvsend.at[t, to, rows], kvrecv.at[t, z, rows], K_KV + t, at(to, k, x, y))

        if offsets is None:
            each_z(send)
        else:
            for dz in offsets:
                send(hop(z, dz, NZ))

    def project_first():
        tokens = [fresh_in[0, 0, k], fresh_in[1, 0, k]]
        project_new(0, tokens)
        q = jnp.zeros((16, 256), jnp.float32)
        for core in (0, 1):
            q += jnp.dot(tokens[core], wq2[core], preferred_element_type=jnp.float32)
        for j in (0, 1):
            kvsend[0, :, 4 + j, :] = q[:, j * HD : (j + 1) * HD]

    def query_first():
        new_pair(0)
        along_z(qall.at[k * 16 + z], qall.at[k * 16 + z], K_Q)

    def query_first_half():
        arrived(qall.at[pl.ds(0, 15)], K_Q)
        half = qall.at[pl.ds(k * 16, 16)]
        remote(half, half, K_QPAIR, sib)

    def query_first_rest():
        arrived(qall.at[pl.ds(0, 16)], K_QPAIR)

    def query_half(t):
        arrived(qrecv.at[t, pl.ds(0, 15)], K_Q + t)
        half = jnp.sum(qrecv[t].astype(jnp.float32), axis=0).astype(jnp.bfloat16)
        qpair[t, k] = half
        remote(qpair.at[t, k], qpair.at[t, k], K_QPAIR + t, sib)
        return half.astype(jnp.float32)

    def query_rest(t):
        arrived(qpair.at[t, 1 - k], K_QPAIR + t)
        for half in (0, 1):
            q = qpair[t, half].astype(jnp.float32)
            for j in (0, 1):
                qall[16 * half : 16 * half + 16, j, :] = q[:, j * HD : (j + 1) * HD]

    def new_pair(t):
        rows = 6 if t == 0 else 4
        kvrecv[t, z] = kvsend[t, z]
        arrived(kvrecv.at[t, pl.ds(0, 15), pl.ds(0, rows)], K_KV + t)
        total = jnp.sum(kvrecv[t, :, 0:rows, :], axis=0).astype(jnp.bfloat16).astype(jnp.float32)
        kvown[t] = total[0:4]
        if t == 0:
            qall[k * 16 + z] = total[4:6]

    scale = HD ** (-0.5)
    sub2 = lax.broadcasted_iota(jnp.int32, (2, 128), 0)

    def new_state(t):
        q2 = qall[k * 16 + z]
        scores = [
            jnp.sum(q2 * kvown[s, 0:2, :], axis=1, keepdims=True) * scale for s in range(t + 1)
        ]
        peak = scores[0]
        for s in scores[1:]:
            peak = jnp.maximum(peak, s)
        mass = jnp.zeros((2, 1), jnp.float32)
        mixed = jnp.zeros((2, HD), jnp.float32)
        for s, score in enumerate(scores):
            w = jnp.exp(score - peak)
            mass += w
            mixed += w * kvown[s, 2:4, :]
        return mixed / mass, peak + jnp.log(mass)

    def slot_state(i):
        rows = pl.ds(i * BLOCK, BLOCK)
        q = qall[owner_ref[i]]
        spot = lax.broadcasted_iota(jnp.int32, (8, 256), 1)
        line = lax.broadcasted_iota(jnp.int32, (8, 128), 0)
        q2 = jnp.concatenate(
            [jnp.where(line == j, q[j : j + 1], 0.0).astype(jnp.bfloat16) for j in (0, 1)], axis=1
        )
        scores = lax.dot_general(
            q2, kout[rows, :], (((1,), (1,)), ((), ())), preferred_element_type=jnp.float32
        )
        scores = jnp.where(spot < rows_ref[i], scores * scale, -1e30)
        peak = jnp.max(scores, axis=1, keepdims=True)
        w = jnp.exp(scores - peak)
        mass = jnp.sum(w, axis=1, keepdims=True)
        mixed = jnp.dot(w.astype(jnp.bfloat16), vout[rows, :], preferred_element_type=jnp.float32)
        mixed = mixed / mass
        lse = peak + jnp.log(mass)
        return jnp.where(sub2 == 0, mixed[0:2, :HD], mixed[0:2, HD:]), lse[0:2]

    def exchange_states(t):
        tag = []
        for i in range(3):
            if i == 2 and t == 1:
                new_pair(1)
            mixed, lse = slot_state(i) if i < 2 else new_state(t)
            states[t, k, z, 2 * i : 2 * i + 2, :] = mixed
            tag += [lse[0:1], lse[1:2]]
        states[t, k, z, 6:7, :] = tag_row(tag)
        first, second = owner_ref[0].astype(jnp.float32), owner_ref[1].astype(jnp.float32)
        own = (k * 16 + z).astype(jnp.float32)
        states[t, k, z, 7:8, :] = tag_row([first, first, second, second, own, own, -1.0, -1.0])
        along_z(states.at[t, k, z], states.at[t, k, z], K_STATE + t)
        arrived(states.at[t, k, pl.ds(0, 15)], K_STATE + t)
        remote(states.at[t, k], states.at[t, k], K_STATEPAIR + t, sib)
        arrived(states.at[t, 1 - k], K_STATEPAIR + t)

    def attention(t, first, count):
        held = states[t].reshape(256, 128)
        total = [jnp.sum(states[t, core], axis=0) for core in (0, 1)]
        lse = jnp.concatenate([total[0][6:7], total[1][6:7]], axis=1)
        owner = jnp.concatenate([total[0][7:8], total[1][7:8]], axis=1)
        spot = lax.broadcasted_iota(jnp.int32, (count, 256), 1)
        conv = (lax.broadcasted_iota(jnp.int32, (count, 256), 0) + first).astype(jnp.float32)
        mine_ = owner == conv
        held = held.astype(jnp.bfloat16)
        parts = []
        for j in (0, 1):
            valid = mine_ & (lax.rem(spot, 2) == j)
            kept = jnp.where(valid, lse, -1e30)
            peak = jnp.max(kept, axis=1, keepdims=True)
            w = jnp.where(valid, jnp.exp(kept - peak), 0.0)
            w = w / jnp.sum(w, axis=1, keepdims=True)
            parts.append(
                jnp.dot(w.astype(jnp.bfloat16), held, preferred_element_type=jnp.float32)
            )
        return jnp.concatenate(parts, axis=1).astype(jnp.bfloat16)

    def plane(pick, dst, kind):
        def one(i, carry):
            dx, dy = 2 - i // NY, 2 - lax.rem(i, NY)
            to = hop(x, dx, NX) * NY + hop(y, dy, NY)

            @pl.when(to != me)
            def _():
                remote(pick(to), dst, kind, at(z, k, to // NY, lax.rem(to, NY)))

            return carry

        lax.fori_loop(0, NX * NY, one, 0)

    def next_tokens():
        half = attention(0, 16 * k, 16)
        for core in (0, 1):
            part = jnp.dot(half, wo2[core], preferred_element_type=jnp.float32).astype(jnp.bfloat16)
            osend[core] = part
            orecv[me, core] = part
        plane(lambda to: osend, orecv.at[me], K_OUT)
        arrived(orecv.at[pl.ds(0, 15)], K_OUT)
        tokens = []
        for core in (0, 1):
            out = jnp.sum(orecv[:, core].astype(jnp.float32), axis=0).astype(jnp.bfloat16)
            opair[k, core] = out
            tokens.append(
                (fresh_in[core, 1, k].astype(jnp.float32) + out.astype(jnp.float32)).astype(
                    jnp.bfloat16
                )
            )
        return tokens

    def own_columns(value, width, start):
        pick = lax.broadcasted_iota(jnp.int32, (16, width), 1) == (
            lax.broadcasted_iota(jnp.int32, (16, width), 0) + start
        )
        return lax.dot_general(
            pick.astype(jnp.bfloat16), value, (((1,), (1,)), ((), ())),
            preferred_element_type=jnp.float32,
        ).astype(jnp.bfloat16)

    def last_output():
        both = attention(1, 0, 32)
        part = jnp.dot(both, wo2[k], preferred_element_type=jnp.float32).astype(jnp.bfloat16)
        for side in (0, 1):
            fsend[side] = part[:, side * 128 : (side + 1) * 128]
        frecv[me] = fsend[me // 8]
        plane(lambda to: fsend.at[to // 8], frecv.at[me], K_LAST)
        out_ref[0] = own_columns(
            jnp.concatenate([opair[0, k], opair[1, k]], axis=0), 256, me * 16
        )
        arrived(frecv.at[pl.ds(0, 15)], K_LAST)
        out = jnp.sum(frecv[...].astype(jnp.float32), axis=0).astype(jnp.bfloat16)
        out_ref[1] = own_columns(out, 128, lax.rem(me, 8) * 16)

    for chunk in (0, 1):
        acc[chunk] = jnp.zeros(acc.shape[1:], jnp.float32)
    settled = -1
    done = -1
    for tick in range(NZ):
        if tick == 0:
            for chunk in (0, 1):
                for part in (0, 1):
                    for sign in (1, -1):
                        ring(0, chunk, part, zn[sign])
                hidden_slot(1 + chunk, False)
            hidden_slot(3, False)
            share_tick(0)
            pair_start()
        else:
            if tick == NZ - 1:
                settled += 1
                weight_settle(settled)
                products(done, tick - 1)
                done = tick - 1
            weight_slot(2 * tick - 1)
            if tick <= NZ // 2:
                hello()
            hidden_slot(tick, True)
            if tick + AHEAD < NZ:
                hidden_slot(tick + AHEAD, False)
            weight_slot(2 * tick)
            if tick <= NZ // 2:
                heard()
            share_tick(tick)
        if tick == 2:
            for copy in local:
                copy.wait()
            pair_finish()
            weight_settle(0)
            settled = 0
            project_first()
        if 3 <= tick <= NZ // 2:
            away = range(1, 4) if tick == 3 else (tick,)
            send_new(0, [dz for dz in Z_FAR_FIRST if abs(dz) in away])
        if tick == 11:
            query_first()
        if tick == 14:
            query_first_half()
        if tick in PRODUCT_TICKS:
            upto = tick - 1
            while settled < NZ // 2 and min(2 * (settled + 1), NZ - 1) <= upto:
                settled += 1
                weight_settle(settled)
            products(done, upto)
            done = upto
    last_products()
    query_first_rest()
    for slot in (0, 1):
        rows = pl.ds(slot * BLOCK, BLOCK)
        keep = lax.broadcasted_iota(jnp.int32, (BLOCK, BLOCK), 0) < rows_ref[slot]
        for chunk, out in ((0, kout), (1, vout)):
            out[rows, :] = jnp.where(keep, acc[chunk, rows, :], 0.0).astype(jnp.bfloat16)
    outs = [
        pltpu.make_async_copy(kout, key_ref, osem.at[0]),
        pltpu.make_async_copy(vout, value_ref, osem.at[1]),
    ]
    for copy in outs:
        copy.start()
    exchange_states(0)
    tokens = next_tokens()
    project_query(1, tokens)
    send_query(1)
    project_new(1, tokens)
    send_new(1)
    remote(opair.at[k, 1 - k], opair.at[k, 1 - k], K_OPAIR, sib)
    query_half(1)
    departed(qall.at[pl.ds(0, 15)], K_Q)
    departed(qall.at[pl.ds(0, 16)], K_QPAIR)
    query_rest(1)
    exchange_states(1)
    arrived(opair.at[1 - k, k], K_OPAIR)
    last_output()

    pltpu.make_async_copy(hbuf.at[pl.ds(0, 15)], hbuf.at[pl.ds(0, 15)], hsend).wait()
    pltpu.make_async_copy(wbuf.at[pl.ds(0, 15)], wbuf.at[pl.ds(0, 15)], wsend).wait()
    pltpu.make_async_copy(wbuf.at[pl.ds(0, 16)], wbuf.at[pl.ds(0, 16)], sibsend).wait()
    departed(fresh_in.at[k], K_NEW)
    departed(wq2.at[k], K_WQ)
    departed(wo2.at[k], K_WO)
    departed(opair.at[k, 1 - k], K_OPAIR)
    departed(kvrecv.at[0, pl.ds(0, 15), pl.ds(0, 6)], K_KV)
    departed(qrecv.at[1, pl.ds(0, 15)], K_Q + 1)
    departed(kvrecv.at[1, pl.ds(0, 15), pl.ds(0, 4)], K_KV + 1)
    departed(qpair.at[1, k], K_QPAIR + 1)
    for t in (0, 1):
        departed(states.at[t, k, pl.ds(0, 15)], K_STATE + t)
        departed(states.at[t, k], K_STATEPAIR + t)
    departed(orecv.at[pl.ds(0, 15)], K_OUT)
    departed(frecv.at[pl.ds(0, 15)], K_LAST)
    for copy in outs:
        copy.wait()


def layer(hidden, slot_owner, slot_rows, new_hidden, w_query, w_key, w_value, w_out):
    rows, width = hidden.shape
    cols = w_key.shape[1]
    bf16, f32 = jnp.bfloat16, jnp.float32
    any_ = pl.BlockSpec(memory_space=pl.ANY)
    hbm = pl.BlockSpec(memory_space=pltpu.HBM)
    smem = pl.BlockSpec(memory_space=pltpu.SMEM)
    caches = [jax.ShapeDtypeStruct((rows, cols), bf16)] * 2
    dma = pltpu.SemaphoreType.DMA
    return pl.pallas_call(
        layer_kernel,
        out_shape=caches + [jax.ShapeDtypeStruct((STEPS, 16, 32), bf16)],
        in_specs=[smem, smem] + [hbm] * 6,
        out_specs=[any_, any_, pl.BlockSpec(memory_space=pltpu.VMEM)],
        scratch_shapes=[
            pltpu.VMEM((NX * NY, rows, width), bf16),
            pltpu.VMEM((2 * NZ, 2, BLOCK, cols), bf16),
            pltpu.VMEM((2, rows, cols), f32),
            pltpu.VMEM((rows, cols), bf16),
            pltpu.VMEM((rows, cols), bf16),
            pltpu.VMEM((2, STEPS, 2, 16, 256), bf16),
            pltpu.VMEM((2, 256, 256), bf16),
            pltpu.VMEM((2, 256, 256), bf16),
            pltpu.VMEM((STEPS, 16, 256), bf16),
            pltpu.VMEM((STEPS, NZ, 16, 256), bf16),
            pltpu.VMEM((STEPS, 2, 16, 256), bf16),
            pltpu.VMEM((32, 2, 128), f32),
            pltpu.VMEM((STEPS, NZ, 8, 128), f32),
            pltpu.VMEM((STEPS, NZ, 8, 128), f32),
            pltpu.VMEM((STEPS, 4, 128), f32),
            pltpu.VMEM((STEPS, 2, NZ, 8, 128), f32),
            pltpu.VMEM((2, 16, 256), bf16),
            pltpu.VMEM((16, 2, 16, 256), bf16),
            pltpu.VMEM((2, 2, 16, 256), bf16),
            pltpu.VMEM((2, 32, 128), bf16),
            pltpu.VMEM((16, 32, 128), bf16),
            dma, dma((NX * NY, 4)), dma, dma((2 * NZ, 2, 2)), dma, dma((6,)), dma((2,)),
            dma((KINDS,)), dma((KINDS,)), pltpu.SemaphoreType.REGULAR((2,)),
        ],
        compiler_params=pltpu.CompilerParams(
            collective_id=0, has_side_effects=True, vmem_limit_bytes=60 << 20
        ),
        name="layer",
    )(
        slot_owner, slot_rows, hidden, new_hidden.reshape(STEPS, 2, 16, 256),
        w_query, w_key, w_value, w_out,
    )


def solution(mesh):
    in_specs = (
        P("cache", "head"),
        P("cache"),
        P("cache"),
        P(None, None, "cache"),
        P("cache", "head"),
        P("cache", "head"),
        P("cache", "head"),
        P("head", "cache"),
    )
    out_specs = (P("cache", "head"), P("cache", "head"), P(None, None, ("cache", "head")))

    def on_device(*arrays):
        key, value, out = layer(*arrays)
        low, high = jnp.finfo(key.dtype).min, jnp.finfo(key.dtype).max
        return lax.clamp(low, key, high), lax.clamp(low, value, high), jnp.swapaxes(out, 1, 2)

    return jax.shard_map(
        on_device, mesh=mesh, in_specs=in_specs, out_specs=out_specs, check_vma=False
    )
```
